512 devices in a mesh: exp: 4 (over x), imp: 32 (over z, core), wk: 4 (over y).
Axes of the slice: x: 4, y: 4, z: 16, core: 2. Of those that a mesh axis runs over, the one named last changes fastest.
Arguments:
- flows: float32 [4, 2048, 4096], P('wk', 'exp', 'imp'), may hold values from 0.0112 to 284, as said below
- importer_factor: float32 [4096, 256], P('imp'), may hold values from -0.5 to 1.5
- week_factor: float32 [4, 256], P('wk'), may hold values from 0 to 1
Outputs:
- exporter_out: float32 [2048, 256], P('exp')
- importer_out: float32 [4096, 256], P('imp')
- week_out: float32 [4, 256], P('wk')
The draws below stay inside these ranges and needn't reach their ends.
Inputs may be any that keep to these rules, and one draw needn't show every extreme that they name: `flows`: flows are positive.
All inputs are finite; a program needn't handle non-finite values.
Results may differ from the reference program's by a relative error of at most 0.00022.
Values sent between devices are 32-bit elements; how exact they have to be, the bound alone decides.
A program may use at most 64 MiB of HBM per device.

```python
import math
import jax
import jax.numpy as jnp
from jax import lax

R = 256
I = 2048
J = 4096
K = 4


def draw_flows(key, part):
    keys = jax.random.split(key, 4)
    lo = math.log(0.3)
    hi = math.log(3.0)
    rise = math.log(3.0)
    rows = jnp.exp(jax.random.uniform(keys[0], (I,), jnp.float32, lo, hi) + rise * jnp.arange(I, dtype=jnp.float32) / I)
    cols = jnp.exp(jax.random.uniform(keys[1], (J,), jnp.float32, lo, hi) + rise * jnp.arange(J, dtype=jnp.float32) / J)
    weeks = jnp.exp(jax.random.uniform(keys[2], (K,), jnp.float32, math.log(0.5), math.log(2.0)))
    noise = jax.random.uniform(keys[3], (K, I, J), jnp.float32, 0.25, 1.75)
    return weeks[:, None, None] * rows[None, :, None] * cols[None, None, :] * noise


def block_scale(stream_key, extent, cuts, low, top_value):
    loudness, own = 1.0, jax.random.fold_in(stream_key, 6)
    for position, blocks in cuts:
        draws = jnp.exp(jax.random.uniform(jax.random.fold_in(own, position), (blocks,), jnp.float32, low / len(cuts), top_value / len(cuts)))
        loudness = loudness * jnp.repeat(draws, extent[position] // blocks).reshape([-1 if axis == position else 1 for axis in range(len(extent))])
    return loudness


def setup_inputs(seed: int = 0) -> dict:
    arg_keys = jax.random.split(jax.random.key(seed), 4)
    flows = draw_flows(jax.random.fold_in(arg_keys[3], 71), 0)
    importer_factor = jnp.clip(-0.5 + 2.0 * jax.random.uniform(arg_keys[1], (J, R), jnp.float32) ** block_scale(arg_keys[1], (J, R), ((0, 32),), -0.2, 0.2), -0.5, 1.5)
    week_factor = jnp.clip(1.0 * jax.random.uniform(arg_keys[2], (K, R), jnp.float32) ** block_scale(arg_keys[2], (K, R), ((0, 4),), -0.2, 0.2), 0.0, 1.0)
    return {"flows": flows, "importer_factor": importer_factor, "week_factor": week_factor}


ridge = 0.2
eps = 1e-06
hp = lax.Precision.HIGHEST

def solve_rows(m, g1, g2):
    h = g1 * g2
    lam = ridge * jnp.trace(h) / h.shape[0]
    v = h + lam * jnp.eye(h.shape[0], dtype=jnp.float32)
    chol = jnp.linalg.cholesky(v)
    return jax.scipy.linalg.cho_solve((chol, True), m.T).T

def unit_cols(x):
    scale = jnp.sqrt(lax.optimization_barrier(jnp.sum(x * x, 0)) / x.shape[0] + eps)
    y = x / scale
    return (y, jnp.dot(y.T.astype(jnp.float32), y.astype(jnp.float32), precision=hp, preferred_element_type=jnp.float32))

def reference(flows, importer_factor, week_factor):
    row_tot = lax.optimization_barrier(jnp.sum(flows, 2))
    col_tot = lax.optimization_barrier(jnp.sum(flows, 1))
    grand = lax.optimization_barrier(jnp.sum(row_tot, 1))
    resid = flows - row_tot[:, :, None] * col_tot[:, None, :] / grand[:, None, None]
    gram_b = jnp.dot(importer_factor.T.astype(jnp.float32), importer_factor.astype(jnp.float32), precision=hp, preferred_element_type=jnp.float32)
    gram_c = jnp.dot(week_factor.T.astype(jnp.float32), week_factor.astype(jnp.float32), precision=hp, preferred_element_type=jnp.float32)
    inner = jnp.einsum('kij,jr->kir', resid, importer_factor, precision=hp)
    m_a = lax.optimization_barrier(jnp.sum(inner * week_factor[:, None, :], 0))
    fac_a, gram_a = unit_cols(solve_rows(m_a, gram_b, gram_c))
    weighted = fac_a[None, :, :] * week_factor[:, None, :]
    m_b = jnp.einsum('kij,kir->jr', resid, weighted, precision=hp)
    fac_b, gram_b2 = unit_cols(solve_rows(m_b, gram_a, gram_c))
    inner = jnp.einsum('kij,jr->kir', resid, fac_b, precision=hp)
    m_c = lax.optimization_barrier(jnp.sum(inner * fac_a[None, :, :], 1))
    fac_c, unused = unit_cols(solve_rows(m_c, gram_a, gram_b2))
    return (fac_a, fac_b, fac_c)
```

```python
import functools

import jax
import jax.numpy as jnp
from jax import lax
from jax.experimental import pallas as pl
from jax.experimental.pallas import tpu as pltpu
from jax.sharding import PartitionSpec as P

ridge = 0.2
eps = 1e-06
hp = lax.Precision.HIGHEST
f32 = jnp.float32
bf16 = jnp.bfloat16
R = 256
H = 128
MESH = pl.DeviceIdType.MESH
STATS = 4
STEPS = 7


def dot(a, b, ca=1, cb=0):
    return lax.dot_general(a, b, (((ca,), (cb,)), ((), ())), precision=hp, preferred_element_type=f32)


def split(a):
    hi = a.astype(bf16)
    return hi, (a - hi.astype(f32)).astype(bf16)


def dot3(a, b):
    ah, al = a
    bh, bl = b
    d = functools.partial(jnp.dot, preferred_element_type=f32)
    return d(ah, bh) + (d(ah, bl) + d(al, bh))


def eye():
    return (lax.broadcasted_iota(jnp.int32, (R, R), 0) == lax.broadcasted_iota(jnp.int32, (R, R), 1)).astype(f32)


def inverse_start(h, diag_sum):
    lam = ridge * diag_sum / R
    one = eye()
    v = h + lam * one
    top = 1.0 + R / ridge
    alpha = 2.0 / (lam * (1.0 + top))
    delta = (top - 1.0) / (top + 1.0)
    e = one - alpha * v
    x = None
    return [v, e, x, alpha, delta, one]


def inverse_steps(state, n):
    v, e, x, alpha, delta, one = state
    for _ in range(n):
        c = 2.0 / (2.0 - delta * delta)
        delta = delta * delta / (2.0 - delta * delta)
        se = split(e)
        if x is None:
            x = (c * alpha) * (one + e)
        else:
            x = c * (x + dot3(split(x), se))
        e = c * dot3(se, se) + (1.0 - c) * one
    return [v, e, x, alpha, delta, one]


def inverse_end(state):
    v, e, x, alpha, delta, one = state
    for _ in range(2):
        r = one - dot(v, x)
        x = x + dot3(split(x), split(r))
    return x


def kernel(ne, nz, nk, f_ref, b_ref, w_ref, a_out, b_out, c_out,
           u, c_in, y_in, z_in, ma, cx, wx,
           cs, ci, zs, zi, za, xs, ax, ag, mbp, mi, mo, res,
           ssem, rsem):
    e = lax.axis_index("exp")
    p = lax.axis_index("imp")
    k = lax.axis_index("wk")
    z = lax.div(p, 2)
    c = lax.rem(p, 2)
    o = 1 - c
    nq = ne * nk
    q = e * nk + k
    ri = f_ref.shape[1]
    rj = f_ref.shape[2]
    gs = R // nq
    cr = gs // nz
    yc = ri // nk
    zc = yc // nz
    jc = rj // nq
    used = [0]
    pending = []

    def take(n):
        base = used[0]
        used[0] += n
        return base

    def remote(src, dst, s, dev):
        return pltpu.make_async_remote_copy(
            src_ref=src, dst_ref=dst, send_sem=ssem.at[s], recv_sem=rsem.at[s],
            device_id=dev, device_id_type=MESH)

    core_dev = {"imp": z * 2 + o}

    def push_core(src, dst):
        cp = remote(src, dst, take(1), core_dev)
        cp.start()
        pending.append(cp.wait_send)
        return cp.wait_recv

    def push_group(n, dev, src, dst, back):
        base = take(n)

        def go(d, carry):
            remote(src(d), dst, base + d, dev(d)).start()
            return carry

        def sent(d, carry):
            remote(src(d), dst, base + d, dev(d)).wait_send()
            return carry

        def arrived(d, carry):
            remote(back(d), back(d), base + d, dev(d)).wait_recv()
            return carry

        lax.fori_loop(1, n, go, 0)
        pending.append(lambda: lax.fori_loop(1, n, sent, 0))
        return lambda: lax.fori_loop(1, n, arrived, 0)

    def zto(d):
        return lax.rem(z + d, nz)

    def zfrom(d):
        return lax.rem(z - d + nz, nz)

    def zdev(d):
        return {"imp": zto(d) * 2 + c}

    def yto(d):
        return lax.rem(k + d, nk)

    def yfrom(d):
        return lax.rem(k - d + nk, nk)

    def ydev(d):
        return {"wk": yto(d)}

    def xto(d):
        return lax.rem(e + d, ne)

    def xfrom(d):
        return lax.rem(e - d + ne, ne)

    def xdev(d):
        return {"exp": xto(d)}

    def qto(d):
        return lax.rem(q + d, nq)

    def qfrom(d):
        return lax.rem(q - d + nq, nq)

    def qdev(d):
        return {"exp": lax.div(qto(d), nk), "wk": lax.rem(qto(d), nk)}

    barrier = pltpu.get_barrier_semaphore()
    pl.semaphore_signal(barrier, inc=1, device_id=core_dev, device_id_type=MESH)

    def greet_z(d, carry):
        pl.semaphore_signal(barrier, inc=1, device_id=zdev(d), device_id_type=MESH)
        return carry

    def greet_q(d, carry):
        pl.semaphore_signal(barrier, inc=1, device_id=qdev(d), device_id_type=MESH)
        return carry

    lax.fori_loop(1, nz, greet_z, 0)
    lax.fori_loop(1, nq, greet_q, 0)

    def chain_fill(n, gram, stats):
        for h in range(2):
            u_g = gram[:, h * H:(h + 1) * H]
            mbp[h, :, :] = u_g
            cs[n, h, pl.ds(0, gs), :] = mbp[h, pl.ds(pl.multiple_of(q * gs, gs), gs), :]
            for s, row in enumerate(stats):
                cs[n, h, gs + s:gs + s + 1, :] = row[:, h * H:(h + 1) * H]
            for s in range(len(stats), STATS):
                cs[n, h, gs + s:gs + s + 1, :] = jnp.zeros((1, H), f32)

    def chain_core(n):
        return push_core(cs.at[n, o], ci.at[n])

    def chain_z1(n):
        t = cs[n, c] + ci[n]
        for i in range(nz):
            zs[n, i, 0:cr, :] = t[i * cr:(i + 1) * cr]
            s = gs + i % STATS
            zs[n, i, cr:cr + 1, :] = t[s:s + 1]
        zi[n, z, :, :] = zs[n, z]
        return push_group(nz, zdev, lambda d: zs.at[n, zto(d)], zi.at[n, z], lambda d: zi.at[n, zfrom(d)])

    def chain_z2(n):
        za[n, z, :, :] = jnp.sum(zi[n], axis=0)
        return push_group(nz, zdev, lambda d: za.at[n, z], za.at[n, z], lambda d: za.at[n, zfrom(d)])

    def chain_q(n):
        for i in range(nz):
            xs[n, c, q, i * cr:(i + 1) * cr, :] = za[n, i, 0:cr, :]
        for s in range(STATS):
            xs[n, c, q, gs + s:gs + s + 1, :] = za[n, s, cr:cr + 1, :]
        return push_group(nq, qdev, lambda d: xs.at[n, c, q], xs.at[n, c, q], lambda d: xs.at[n, c, qfrom(d)])

    def chain_back(n):
        return push_core(xs.at[n, c], xs.at[n, c])

    def chain_gram(n):
        return jnp.concatenate([xs[n, h, :, 0:gs, :].reshape(R, H) for h in range(2)], axis=1)

    def chain_stat(n, qq, s):
        return jnp.concatenate([xs[n, h, qq, gs + s:gs + s + 1, :] for h in range(2)], axis=1)

    def chain_week(n, kk, s):
        tot = chain_stat(n, kk, s)
        for ee in range(1, ne):
            tot = tot + chain_stat(n, ee * nk + kk, s)
        return tot

    f = f_ref[0]
    b = b_ref[...]
    w = w_ref[...]
    rowp = dot(jnp.ones((8, rj), f32), f, 1, 1)
    colp = jnp.sum(f, axis=0, keepdims=True)
    g = dot(f, b - 0.5)
    v = jnp.sum(g, axis=0, keepdims=True)
    gw = g * w
    u[0, :, :] = gw[:, 0:H]
    u[1, :, :] = gw[:, H:R]
    rows = [rowp[0:1, i * R:(i + 1) * R] for i in range(ri // R)]
    chain_fill(0, dot(b, b, 0, 0), [v, jnp.concatenate([colp, jnp.zeros((1, R - rj), f32)], axis=1)] + rows)
    cx[e, :, :] = colp
    wx[k, :, :] = w

    pl.semaphore_wait(barrier, 1 + (nz - 1) + (nq - 1))

    w_cs = chain_core(0)
    w_u = push_core(u.at[o], c_in)
    w_w = push_group(nk, ydev, lambda d: wx.at[k], wx.at[k], lambda d: wx.at[yfrom(d)])
    w_c = push_group(ne, xdev, lambda d: cx.at[e], cx.at[e], lambda d: cx.at[xfrom(d)])

    w_cs()
    w_z1 = chain_z1(0)
    w_u()
    u[c, :, :] = u[c] + c_in[...]
    y_in[k, :, :] = u[c, pl.ds(pl.multiple_of(k * yc, yc), yc), :]
    w_y = push_group(nk, ydev, lambda d: u.at[c, pl.ds(pl.multiple_of(yto(d) * yc, yc), yc)],
                     y_in.at[k], lambda d: y_in.at[yfrom(d)])
    w_z1()
    w_z2 = chain_z2(0)
    w_y()
    y_in[0, :, :] = jnp.sum(y_in[...], axis=0)
    z_in[z, :, :] = y_in[0, pl.ds(pl.multiple_of(z * zc, zc), zc), :]
    w_z3 = push_group(nz, zdev, lambda d: y_in.at[0, pl.ds(pl.multiple_of(zto(d) * zc, zc), zc)],
                      z_in.at[z], lambda d: z_in.at[zfrom(d)])
    w_z2()
    w_q = chain_q(0)

    def tile(zz):
        return ma.at[c, pl.ds(pl.multiple_of(k * yc + zz * zc, zc), zc)]

    def part(kk):
        return ma.at[c, pl.ds(pl.multiple_of(kk * yc, yc), yc)]

    w_z3()
    tile(z)[...] = jnp.sum(z_in[...], axis=0)
    w_z4 = push_group(nz, zdev, lambda d: tile(z), tile(z), lambda d: tile(zfrom(d)))
    w_w()
    ws = jnp.concatenate([wx[i] for i in range(nk)] + [jnp.zeros((8 - nk, R), f32)], axis=0)
    gram_c = dot(ws, ws, 0, 0)
    w_q()
    w_b = chain_back(0)
    w_z4()
    w_y2 = push_group(nk, ydev, lambda d: part(k), part(k), lambda d: part(yfrom(d)))
    w_b()
    h1 = chain_gram(0) * gram_c
    one = eye()
    inv = inverse_steps(inverse_start(h1, jnp.sum(h1 * one)), 3)
    w_y2()
    w_m = push_core(ma.at[c], ma.at[c])

    w_c()
    col = cx[0]
    for i in range(1, ne):
        col = col + cx[i]
    zero = jnp.zeros((1, R), f32)
    coef, totals = [], []
    for kk in range(nk):
        grand = jnp.sum(chain_week(0, kk, 1))
        coef.append(chain_week(0, kk, 0) * ws[kk:kk + 1] / grand)
        totals.append(jnp.concatenate([chain_stat(0, e * nk + kk, 2 + i) for i in range(ri // R)], axis=1))
    coef = jnp.concatenate(coef + [zero] * (8 - nk), axis=0)
    totals = jnp.concatenate(totals + [jnp.zeros((1, ri), f32)] * (8 - nk), axis=0)
    mine = (lax.broadcasted_iota(jnp.int32, (8, 1), 0) == k).astype(f32)
    grand = jnp.zeros((1, 1), f32)
    for ee in range(ne):
        grand = grand + jnp.sum(chain_stat(0, ee * nk + k, 1), axis=1, keepdims=True)
    res[...] = f - dot(totals * mine, (col / grand) * mine, 0, 0)

    inv = inverse_steps(inv, STEPS - 3)
    x1 = inverse_end(inv)
    w_m()
    m_a = jnp.concatenate([ma[0], ma[1]], axis=1) - dot(totals, coef, 0, 0)
    raw_a = dot(m_a, x1)
    a_out[...] = raw_a

    gram = dot(raw_a, raw_a, 0, 0)
    mbp[0, :, :] = gram[:, 0:H]
    mbp[1, :, :] = gram[:, H:R]
    gr = R // nk
    ax[e, :, :] = mbp[c, pl.ds(pl.multiple_of(k * gr, gr), gr), :]
    w_ax = push_group(ne, xdev, lambda d: ax.at[e], ax.at[e], lambda d: ax.at[xfrom(d)])

    t = dot(res[...], raw_a, 0, 0)
    tw = t * w
    for i in range(nq):
        mo[0, i, :, :] = tw[i * jc:(i + 1) * jc]
    mi[q, :, :] = mo[0, q]
    w_mi = push_group(nq, qdev, lambda d: mo.at[0, qto(d)], mi.at[q], lambda d: mi.at[qfrom(d)])

    def gpart(kk):
        return ag.at[c, pl.ds(pl.multiple_of(kk * gr, gr), gr)]

    w_ax()
    gpart(k)[...] = jnp.sum(ax[...], axis=0)
    w_ag = push_group(nk, ydev, lambda d: gpart(k), gpart(k), lambda d: gpart(yfrom(d)))
    w_mi()
    mo[1, q, :, :] = jnp.sum(mi[...], axis=0)
    w_mo = push_group(nq, qdev, lambda d: mo.at[1, q], mo.at[1, q], lambda d: mo.at[1, qfrom(d)])
    w_ag()
    w_ac = push_core(ag.at[c], ag.at[c])
    w_ac()
    gram_a = jnp.concatenate([ag[0], ag[1]], axis=1)

    def unscale(gram, count):
        d = gram * one
        inv_row = 1.0 / jnp.sqrt(jnp.sum(d, axis=0, keepdims=True) / count + eps)
        inv_col = 1.0 / jnp.sqrt(jnp.sum(d, axis=1, keepdims=True) / count + eps)
        return inv_row, gram * inv_row * inv_col

    sa, gram_a = unscale(gram_a, ri * ne)
    h2 = gram_a * gram_c
    inv = inverse_steps(inverse_start(h2, jnp.sum(h2 * one)), STEPS)
    x2 = inverse_end(inv)
    a_out[...] = a_out[...] * sa
    w_mo()
    m_b = mo[1].reshape(rj, R) * sa
    raw_b = dot(m_b, x2)

    chain_fill(1, dot(raw_b, raw_b, 0, 0), [jnp.sum(t * raw_b, axis=0, keepdims=True)])
    w_cs = chain_core(1)
    w_cs()
    w_z1 = chain_z1(1)
    w_z1()
    w_z2 = chain_z2(1)
    w_z2()
    w_q = chain_q(1)
    w_q()
    w_b = chain_back(1)
    w_b()
    sb, gram_b2 = unscale(chain_gram(1), rj * nz * 2)
    b_out[...] = raw_b * sb
    h3 = gram_a * gram_b2
    inv = inverse_steps(inverse_start(h3, jnp.sum(h3 * one)), STEPS)
    x3 = inverse_end(inv)
    m_c = jnp.concatenate([chain_week(1, kk, 0) * sa * sb for kk in range(nk)] + [zero] * (8 - nk), axis=0)
    raw_c = dot(m_c, x3)
    sc = jnp.sqrt(jnp.sum(raw_c * raw_c, axis=0, keepdims=True) / nk + eps)
    c_out[...] = jnp.sum(raw_c * mine, axis=0, keepdims=True) / sc

    for fin in pending:
        fin()


def per_device(ne, nz, nk, flows, importer_factor, week_factor):
    ri, rj = flows.shape[1], flows.shape[2]
    nq = ne * nk
    gs = R // nq
    cr = gs // nz
    yc = ri // nk
    vm = functools.partial(pltpu.VMEM, dtype=f32)
    nsem = 512
    return pl.pallas_call(
        functools.partial(kernel, ne, nz, nk),
        out_shape=(
            jax.ShapeDtypeStruct((ri, R), f32),
            jax.ShapeDtypeStruct((rj, R), f32),
            jax.ShapeDtypeStruct((1, R), f32),
        ),
        in_specs=[pl.BlockSpec(memory_space=pltpu.VMEM)] * 3,
        out_specs=[pl.BlockSpec(memory_space=pltpu.VMEM)] * 3,
        scratch_shapes=[
            vm((2, ri, H)),
            vm((ri, H)),
            vm((nk, yc, H)),
            vm((nz, yc // nz, H)),
            vm((2, ri, H)),
            vm((ne, 1, rj)),
            vm((nk, 1, R)),
            vm((2, 2, gs + STATS, H)),
            vm((2, gs + STATS, H)),
            vm((2, nz, cr + 1, H)),
            vm((2, nz, cr + 1, H)),
            vm((2, nz, cr + 1, H)),
            vm((2, 2, nq, gs + STATS, H)),
            vm((ne, R // nk, H)),
            vm((2, R, H)),
            vm((2, R, H)),
            vm((nq, rj // nq, R)),
            vm((2, nq, rj // nq, R)),
            vm((ri, rj)),
            pltpu.SemaphoreType.DMA((nsem,)),
            pltpu.SemaphoreType.DMA((nsem,)),
        ],
        compiler_params=pltpu.CompilerParams(
            collective_id=0, has_side_effects=True, vmem_limit_bytes=48 * 1024 * 1024
        ),
    )(flows, importer_factor, week_factor)


def solution(mesh):
    in_specs = (P("wk", "exp", "imp"), P("imp", None), P("wk", None))
    out_specs = (P("exp", None), P("imp", None), P("wk", None))
    fn = functools.partial(per_device, mesh.shape["exp"], mesh.shape["imp"] // 2, mesh.shape["wk"])
    return jax.shard_map(fn, mesh=mesh, in_specs=in_specs, out_specs=out_specs, check_vma=False)
```

```python
import functools

import jax
import jax.numpy as jnp
from jax import lax
from jax.experimental import pallas as pl
from jax.experimental.pallas import tpu as pltpu
from jax.sharding import PartitionSpec as P

ridge = 0.2
eps = 1e-06
hp = lax.Precision.HIGHEST
f32 = jnp.float32
bf16 = jnp.bfloat16
R = 256
H = 128
MESH = pl.DeviceIdType.MESH
STATS = 5
STEPS = 7


def dot(a, b, ca=1, cb=0):
    return lax.dot_general(a, b, (((ca,), (cb,)), ((), ())), precision=hp, preferred_element_type=f32)


def split(a):
    hi = a.astype(bf16)
    return hi, (a - hi.astype(f32)).astype(bf16)


def dot3(a, b):
    ah, al = a
    bh, bl = b
    d = functools.partial(jnp.dot, preferred_element_type=f32)
    return d(ah, bh) + (d(ah, bl) + d(al, bh))


def eye():
    return (lax.broadcasted_iota(jnp.int32, (R, R), 0) == lax.broadcasted_iota(jnp.int32, (R, R), 1)).astype(f32)


def inverse_start(h, diag_sum):
    lam = ridge * diag_sum / R
    one = eye()
    v = h + lam * one
    top = 1.0 + R / ridge
    alpha = 2.0 / (lam * (1.0 + top))
    delta = (top - 1.0) / (top + 1.0)
    e = one - alpha * v
    x = None
    return [v, e, x, alpha, delta, one]


def inverse_steps(state, n):
    v, e, x, alpha, delta, one = state
    for _ in range(n):
        c = 2.0 / (2.0 - delta * delta)
        delta = delta * delta / (2.0 - delta * delta)
        se = split(e)
        if x is None:
            x = (c * alpha) * (one + e)
        else:
            x = c * (x + dot3(split(x), se))
        e = c * dot3(se, se) + (1.0 - c) * one
    return [v, e, x, alpha, delta, one]


def inverse_end(state):
    v, e, x, alpha, delta, one = state
    for _ in range(2):
        r = one - dot(v, x)
        x = x + dot3(split(x), split(r))
    return x


def triangle():
    r = lax.broadcasted_iota(jnp.int32, (H, H), 0)
    c = lax.broadcasted_iota(jnp.int32, (H, H), 1)
    return r, c


def pack(g):
    r, c = triangle()
    g11 = g[H:, H:]
    return jnp.where(r <= c, g[:H, :H], g11), g[:H, H:], jnp.sum(jnp.where(r == c, g11, 0.0), axis=0, keepdims=True)


def unpack(p0, p1, d):
    r, c = triangle()
    g00 = jnp.where(r <= c, p0, 0.0) + jnp.where(r < c, p0, 0.0).T
    low = jnp.where(r > c, p0, 0.0)
    g11 = low + low.T + jnp.where(r == c, d, 0.0)
    return jnp.concatenate(
        [jnp.concatenate([g00, p1], axis=1), jnp.concatenate([p1.T, g11], axis=1)], axis=0)


def kernel(ne, nz, nk, f_hbm, b_hbm, w_hbm, a_out, b_out, c_out,
           f_ref, b_ref, w_ref, fa, u, c_in, z_in, ma, cq, wx,
           pk, cs, ci, zi, xs, gi, gx, gag, mi, mo, mos, res, raw,
           ssem, rsem, lsem):
    e = lax.axis_index("exp")
    p = lax.axis_index("imp")
    k = lax.axis_index("wk")
    z = lax.div(p, 2)
    c = lax.rem(p, 2)
    o = 1 - c
    nq = ne * nk
    q = e * nk + k
    ri, rj = f_ref.shape
    yc = ri // nk
    zc = yc // nz
    jc = rj // nq
    gs = H // nq
    used = [0]
    pending = []

    loads = [pltpu.make_async_copy(f_hbm.at[0], f_ref, lsem.at[0]),
             pltpu.make_async_copy(b_hbm, b_ref, lsem.at[1]),
             pltpu.make_async_copy(w_hbm, w_ref, lsem.at[2])]
    for cp in loads:
        cp.start()

    def take():
        used[0] += 1
        return used[0] - 1

    def remote(src, dst, s, dev):
        return pltpu.make_async_remote_copy(
            src_ref=src, dst_ref=dst, send_sem=ssem.at[s], recv_sem=rsem.at[s],
            device_id=dev, device_id_type=MESH)

    core_dev = {"imp": z * 2 + o}

    def push_core(src, dst):
        cp = remote(src, dst, take(), core_dev)
        cp.start()
        pending.append(cp.wait_send)
        return cp.wait_recv

    def push_group(n, dev, src, dst, every):
        s = take()

        def go(d, carry):
            remote(src(d), dst, s, dev(d)).start()
            return carry

        lax.fori_loop(1, n, go, 0)
        cp = remote(every, every, s, dev(1))
        pending.append(cp.wait_send)
        return cp.wait_recv

    def zto(d):
        return lax.rem(z + d, nz)

    def zdev(d):
        return {"imp": zto(d) * 2 + c}

    def yto(d):
        return lax.rem(k + d, nk)

    def ydev(d):
        return {"wk": yto(d)}

    def qto(d):
        return lax.rem(q + d, nq)

    def qdev(d):
        return {"exp": lax.div(qto(d), nk), "wk": lax.rem(qto(d), nk)}

    barrier = pltpu.get_barrier_semaphore()
    pl.semaphore_signal(barrier, inc=1, device_id=core_dev, device_id_type=MESH)

    def greet_z(d, carry):
        pl.semaphore_signal(barrier, inc=1, device_id=zdev(d), device_id_type=MESH)
        return carry

    def greet_q(d, carry):
        pl.semaphore_signal(barrier, inc=1, device_id=qdev(d), device_id_type=MESH)
        return carry

    lax.fori_loop(1, nz, greet_z, 0)
    lax.fori_loop(1, nq, greet_q, 0)

    def chain_fill(n, gram, stats):
        p0, p1, d = pack(gram)
        pk[0, :, :] = p0
        pk[1, :, :] = p1
        for h in range(2):
            cs[n, h, 0:gs, :] = pk[h, pl.ds(pl.multiple_of(q * gs, gs), gs), :]
            cs[n, h, gs:gs + 1, :] = d
            for s, row in enumerate(stats):
                cs[n, h, gs + 1 + s:gs + 2 + s, :] = row[:, h * H:(h + 1) * H]
            for s in range(len(stats), STATS - 1):
                cs[n, h, gs + 1 + s:gs + 2 + s, :] = jnp.zeros((1, H), f32)

    def chain_core(n):
        return push_core(cs.at[n, o], ci.at[n])

    def chain_z(n):
        zi[n, z, :, :] = cs[n, c] + ci[n]
        return push_group(nz, zdev, lambda d: zi.at[n, z], zi.at[n, z], zi.at[n, pl.ds(0, nz - 1)])

    def chain_q(n):
        xs[n, c, q, :, :] = jnp.sum(zi[n], axis=0)
        return push_group(nq, qdev, lambda d: xs.at[n, c, q], xs.at[n, c, q], xs.at[n, c, pl.ds(0, nq - 1)])

    def chain_back(n):
        return push_core(xs.at[n, c], xs.at[n, c])

    def chain_gram(n):
        return unpack(xs[n, 0, :, 0:gs, :].reshape(H, H), xs[n, 1, :, 0:gs, :].reshape(H, H), xs[n, 0, 0, gs:gs + 1, :])

    def chain_stat(n, qq, s):
        return jnp.concatenate([xs[n, h, qq, gs + 1 + s:gs + 2 + s, :] for h in range(2)], axis=1)

    def add(terms):
        tot = terms[0]
        for term in terms[1:]:
            tot = tot + term
        return tot

    for cp in loads:
        cp.wait()
    f = f_ref[...]
    b = b_ref[...]
    w = w_ref[...]
    shifted = b - 0.5
    wx[k, :, :] = w
    rowp = dot(jnp.ones((8, rj), f32), f, 1, 1)
    colp = jnp.sum(f, axis=0, keepdims=True)
    cq[q, :, :] = colp
    v = dot(jnp.broadcast_to(colp, (8, rj)), shifted)[0:1]
    chain_fill(0, dot(b, b, 0, 0), [v] + [rowp[0:1, i * R:(i + 1) * R] for i in range(ri // R)])
    fa[k, :, :] = f_ref[pl.ds(pl.multiple_of(k * yc, yc), yc), :]

    pl.semaphore_wait(barrier, 1 + (nz - 1) + (nq - 1))

    w_f = push_group(nk, ydev, lambda d: f_ref.at[pl.ds(pl.multiple_of(yto(d) * yc, yc), yc)], fa.at[k], fa.at[pl.ds(0, nk - 1)])
    w_cs = chain_core(0)
    w_w = push_group(nk, ydev, lambda d: wx.at[k], wx.at[k], wx.at[pl.ds(0, nk - 1)])
    w_cs()
    w_z = chain_z(0)
    w_c = push_group(nq, qdev, lambda d: cq.at[q], cq.at[q], cq.at[pl.ds(0, nq - 1)])

    w_w()
    ws = jnp.concatenate([wx[i] for i in range(nk)] + [jnp.zeros((8 - nk, R), f32)], axis=0)
    gram_c = dot(ws, ws, 0, 0)
    w_f()
    g = dot(fa[...].reshape(ri, rj), shifted)
    gw = add([g[i * yc:(i + 1) * yc] * ws[i:i + 1] for i in range(nk)])
    u[0, :, :] = gw[:, 0:H]
    u[1, :, :] = gw[:, H:R]
    w_u = push_core(u.at[o], c_in)
    w_u()
    u[c, :, :] = u[c] + c_in[...]
    z_in[z, :, :] = u[c, pl.ds(pl.multiple_of(z * zc, zc), zc), :]
    w_z3 = push_group(nz, zdev, lambda d: u.at[c, pl.ds(pl.multiple_of(zto(d) * zc, zc), zc)],
                      z_in.at[z], z_in.at[pl.ds(0, nz - 1)])
    w_z()
    w_q = chain_q(0)
    w_z3()
    tile = ma.at[c, pl.ds(pl.multiple_of(z * zc, zc), zc)]
    tile[...] = jnp.sum(z_in[...], axis=0)
    w_z4 = push_group(nz, zdev, lambda d: tile, tile, ma.at[c, pl.ds(0, yc - zc)])
    w_q()
    w_b = chain_back(0)
    w_b()
    h1 = chain_gram(0) * gram_c
    one = eye()
    inv = inverse_steps(inverse_start(h1, jnp.sum(h1 * one)), STEPS)
    x1 = inverse_end(inv)

    w_c()
    zero = jnp.zeros((1, R), f32)
    pad = [jnp.zeros((1, H), f32)] * (8 - nk)
    seg, half = lax.div(k, 2), lax.rem(k, 2)
    coef, totals, cols = [], [], []
    for kk in range(nk):
        grand = add([jnp.sum(chain_stat(0, ee * nk + kk, 1 + i), axis=1, keepdims=True)
                     for ee in range(ne) for i in range(ri // R)])
        coef.append(add([chain_stat(0, ee * nk + kk, 0) for ee in range(ne)]) * ws[kk:kk + 1] / grand)
        totals.append(xs[0, half, e * nk + kk, pl.ds(gs + 2 + seg, 1), :])
        cols.append(add([cq[ee * nk + kk] for ee in range(ne)]) / grand)
    coef = jnp.concatenate(coef + [zero] * (8 - nk), axis=0)
    totals = jnp.concatenate(totals + pad, axis=0)
    week = lax.broadcasted_iota(jnp.int32, (8, 1), 0)
    for kk in range(nk):
        only = (week == kk).astype(f32)
        res[:, kk * rj:(kk + 1) * rj] = fa[kk] - dot(totals * only, cols[kk] * only, 0, 0)
    fix = dot(totals, coef, 0, 0)

    w_z4()
    w_m = push_core(ma.at[c], ma.at[c])
    w_m()
    raw_a = dot(jnp.concatenate([ma[0], ma[1]], axis=1) - fix, x1)

    p0, p1, d = pack(dot(raw_a, raw_a, 0, 0))
    pk[0, :, :] = p0
    pk[1, :, :] = p1
    for i in range(nq):
        gx[i, 0:gs, :] = pk[c, i * gs:(i + 1) * gs, :]
        gx[i, gs:gs + 1, :] = d
    gi[q, :, :] = gx[q]
    w_gi = push_group(nq, qdev, lambda d: gx.at[qto(d)], gi.at[q], gi.at[pl.ds(0, nq - 1)])

    t = dot(res[...], raw_a, 0, 0)
    tw = add([t[i * rj:(i + 1) * rj] * ws[i:i + 1] for i in range(nk)])
    for i in range(nq):
        mos[i, :, :] = tw[i * jc:(i + 1) * jc]
    mi[q, :, :] = mos[q]
    w_mi = push_group(nq, qdev, lambda d: mos.at[qto(d)], mi.at[q], mi.at[pl.ds(0, nq - 1)])
    raw[0, k, :, :] = raw_a[:, 0:H]
    raw[1, k, :, :] = raw_a[:, H:R]

    w_gi()
    gsum = jnp.sum(gi[...], axis=0)
    mine = gag.at[c, pl.ds(pl.multiple_of(q * gs, gs), gs)]
    mine[...] = gsum[0:gs]
    w_ga = push_group(nq, qdev, lambda d: mine, mine, gag.at[c, pl.ds(0, H - gs)])
    w_mi()
    mo[q, :, :] = jnp.sum(mi[...], axis=0)
    w_mo = push_group(nq, qdev, lambda d: mo.at[q], mo.at[q], mo.at[pl.ds(0, nq - 1)])
    w_ga()
    w_gc = push_core(gag.at[c], gag.at[c])
    w_raw = push_group(nk, ydev, lambda d: raw.at[c, k], raw.at[c, k], raw.at[c, pl.ds(0, nk - 1)])
    w_gc()
    gram_a = unpack(gag[0], gag[1], gsum[gs:gs + 1])

    def unscale(gram, count):
        d = gram * one
        inv_row = 1.0 / jnp.sqrt(jnp.sum(d, axis=0, keepdims=True) / count + eps)
        inv_col = 1.0 / jnp.sqrt(jnp.sum(d, axis=1, keepdims=True) / count + eps)
        return inv_row, gram * inv_row * inv_col

    sa, gram_a = unscale(gram_a, ri * ne)
    h2 = gram_a * gram_c
    x2 = inverse_end(inverse_steps(inverse_start(h2, jnp.sum(h2 * one)), STEPS))
    w_mo()
    raw_b = dot(mo[...].reshape(rj, R) * sa, x2)

    chain_fill(1, dot(raw_b, raw_b, 0, 0),
               [jnp.sum(t[i * rj:(i + 1) * rj] * raw_b, axis=0, keepdims=True) for i in range(nk)])
    w_cs = chain_core(1)
    w_cs()
    w_z = chain_z(1)
    w_raw()
    w_rc = push_core(raw.at[c], raw.at[c])
    w_rc()
    a_out[:, 0:H] = raw[0].reshape(ri, H) * sa[:, 0:H]
    a_out[:, H:R] = raw[1].reshape(ri, H) * sa[:, H:R]
    w_z()
    w_q = chain_q(1)
    w_q()
    w_b = chain_back(1)
    w_b()
    sb, gram_b2 = unscale(chain_gram(1), rj * nz * 2)
    b_out[...] = raw_b * sb
    h3 = gram_a * gram_b2
    x3 = inverse_end(inverse_steps(inverse_start(h3, jnp.sum(h3 * one)), STEPS))
    scale = sa * sb
    m_c = jnp.concatenate([add([chain_stat(1, qq, kk) for qq in range(nq)]) * scale for kk in range(nk)] + [zero] * (8 - nk), axis=0)
    raw_c = dot(m_c, x3)
    sc = jnp.sqrt(jnp.sum(raw_c * raw_c, axis=0, keepdims=True) / nk + eps)
    c_out[...] = jnp.sum(raw_c * (week == k).astype(f32), axis=0, keepdims=True) / sc

    for fin in pending:
        fin()
    assert used[0] == NSEM


NSEM = 22


def per_device(ne, nz, nk, flows, importer_factor, week_factor):
    ri, rj = flows.shape[1], flows.shape[2]
    nq = ne * nk
    gs = H // nq
    yc = ri // nk
    vm = functools.partial(pltpu.VMEM, dtype=f32)
    return pl.pallas_call(
        functools.partial(kernel, ne, nz, nk),
        out_shape=(
            jax.ShapeDtypeStruct((ri, R), f32),
            jax.ShapeDtypeStruct((rj, R), f32),
            jax.ShapeDtypeStruct((1, R), f32),
        ),
        in_specs=[pl.BlockSpec(memory_space=pl.ANY)] * 3,
        out_specs=[pl.BlockSpec(memory_space=pltpu.VMEM)] * 3,
        scratch_shapes=[
            vm((ri, rj)),
            vm((rj, R)),
            vm((1, R)),
            vm((nk, yc, rj)),
            vm((2, yc, H)),
            vm((yc, H)),
            vm((nz, yc // nz, H)),
            vm((2, yc, H)),
            vm((nq, 1, rj)),
            vm((nk, 1, R)),
            vm((2, H, H)),
            vm((2, 2, gs + STATS, H)),
            vm((2, gs + STATS, H)),
            vm((2, nz, gs + STATS, H)),
            vm((2, 2, nq, gs + STATS, H)),
            vm((nq, gs + 1, H)),
            vm((nq, gs + 1, H)),
            vm((2, H, H)),
            vm((nq, rj // nq, R)),
            vm((nq, rj // nq, R)),
            vm((nq, rj // nq, R)),
            vm((yc, nk * rj)),
            vm((2, nk, yc, H)),
            pltpu.SemaphoreType.DMA((NSEM,)),
            pltpu.SemaphoreType.DMA((NSEM,)),
            pltpu.SemaphoreType.DMA((3,)),
        ],
        compiler_params=pltpu.CompilerParams(
            collective_id=0, has_side_effects=True, vmem_limit_bytes=60 * 1024 * 1024
        ),
    )(flows, importer_factor, week_factor)


def solution(mesh):
    in_specs = (P("wk", "exp", "imp"), P("imp", None), P("wk", None))
    out_specs = (P("exp", None), P("imp", None), P("wk", None))
    fn = functools.partial(per_device, mesh.shape["exp"], mesh.shape["imp"] // 2, mesh.shape["wk"])
    return jax.shard_map(fn, mesh=mesh, in_specs=in_specs, out_specs=out_specs, check_vma=False)
```

```python
import functools

import jax
import jax.numpy as jnp
from jax import lax
from jax.experimental import pallas as pl
from jax.experimental.pallas import tpu as pltpu
from jax.sharding import PartitionSpec as P

ridge = 0.2
eps = 1e-06
hp = lax.Precision.HIGHEST
f32 = jnp.float32
bf16 = jnp.bfloat16
R = 256
H = 128
MESH = pl.DeviceIdType.MESH
STATS = 5
STEPS = 7


def dot(a, b, ca=1, cb=0):
    return lax.dot_general(a, b, (((ca,), (cb,)), ((), ())), precision=hp, preferred_element_type=f32)


def split(a):
    hi = a.astype(bf16)
    return hi, (a - hi.astype(f32)).astype(bf16)


def dot3(a, b):
    ah, al = a
    bh, bl = b
    d = functools.partial(jnp.dot, preferred_element_type=f32)
    return d(ah, bh) + (d(ah, bl) + d(al, bh))


def eye():
    return (lax.broadcasted_iota(jnp.int32, (R, R), 0) == lax.broadcasted_iota(jnp.int32, (R, R), 1)).astype(f32)


def inverse(h):
    one = eye()
    lam = ridge * jnp.sum(h * one) / R
    v = h + lam * one
    top = 1.0 + R / ridge
    alpha = 2.0 / (lam * (1.0 + top))
    delta = (top - 1.0) / (top + 1.0)
    e = one - alpha * v
    for step in range(STEPS):
        c = 2.0 / (2.0 - delta * delta)
        delta = delta * delta / (2.0 - delta * delta)
        se = split(e)
        x = (c * alpha) * (one + e) if step == 0 else c * (x + dot3(split(x), se))
        if step < STEPS - 1:
            e = c * dot3(se, se) + (1.0 - c) * one
    r = one - dot(v, x)
    return x + dot3(split(x), split(r))


def triangle():
    r = lax.broadcasted_iota(jnp.int32, (H, H), 0)
    c = lax.broadcasted_iota(jnp.int32, (H, H), 1)
    return r, c


def pack(g):
    r, c = triangle()
    g11 = g[H:, H:]
    return jnp.where(r <= c, g[:H, :H], g11), g[:H, H:], jnp.sum(jnp.where(r == c, g11, 0.0), axis=0, keepdims=True)


def unpack(p0, p1, d):
    r, c = triangle()
    g00 = jnp.where(r <= c, p0, 0.0) + jnp.where(r < c, p0, 0.0).T
    low = jnp.where(r > c, p0, 0.0)
    g11 = low + low.T + jnp.where(r == c, d, 0.0)
    return jnp.concatenate(
        [jnp.concatenate([g00, p1], axis=1), jnp.concatenate([p1.T, g11], axis=1)], axis=0)


def kernel(ne, nz, nk, f_hbm, b_hbm, w_hbm, a_hbm, b_out_hbm, c_hbm,
           f_ref, b_ref, w_ref, fa, u, c_in, z_in, ma, cq, wx,
           pk, cs, ci, zi, xs, gi, gx, gag, mi, mo, mos, res, raw, a_out, b_out, c_out,
           ssem, rsem, lsem):
    e = lax.axis_index("exp")
    p = lax.axis_index("imp")
    k = lax.axis_index("wk")
    z = lax.div(p, 2)
    c = lax.rem(p, 2)
    o = 1 - c
    nq = ne * nk
    q = e * nk + k
    ri, rj = f_ref.shape
    yc = ri // nk
    zc = yc // nz
    jc = rj // nq
    gs = H // nq
    used = [0]
    pending = []

    loads = [pltpu.make_async_copy(f_hbm.at[0], f_ref, lsem.at[0]),
             pltpu.make_async_copy(b_hbm, b_ref, lsem.at[1]),
             pltpu.make_async_copy(w_hbm, w_ref, lsem.at[2])]
    for cp in loads:
        cp.start()
    stores = [pltpu.make_async_copy(src, dst, lsem.at[3 + i])
              for i, (src, dst) in enumerate([(a_out, a_hbm), (b_out, b_out_hbm), (c_out, c_hbm)])]

    def take():
        used[0] += 1
        return used[0] - 1

    def remote(src, dst, s, dev):
        return pltpu.make_async_remote_copy(
            src_ref=src, dst_ref=dst, send_sem=ssem.at[s], recv_sem=rsem.at[s],
            device_id=dev, device_id_type=MESH)

    core_dev = {"imp": z * 2 + o}

    def push_core(src, dst):
        cp = remote(src, dst, take(), core_dev)
        cp.start()
        pending.append(cp.wait_send)
        return cp.wait_recv

    def push_group(n, dev, src, dst, every, first=1):
        s = take()

        def go(d, carry):
            remote(src(d), dst, s, dev(d)).start()
            return carry

        lax.fori_loop(first, n, go, 0)
        cp = remote(every, every, s, dev(1))
        pending.append(cp.wait_send)
        return cp.wait_recv

    def zto(d):
        return lax.rem(z + d, nz)

    def zdev(d):
        return {"imp": zto(d) * 2 + c}

    def yto(d):
        return lax.rem(k + d, nk)

    def ydev(d):
        return {"wk": yto(d)}

    def qto(d):
        return lax.rem(q + d, nq)

    def qdev(d):
        return {"exp": lax.div(qto(d), nk), "wk": lax.rem(qto(d), nk)}

    def odev(d):
        return {"exp": lax.div(qto(d), nk), "wk": lax.rem(qto(d), nk), "imp": z * 2 + o}

    barrier = pltpu.get_barrier_semaphore()
    def greet_z(d, carry):
        pl.semaphore_signal(barrier, inc=1, device_id=zdev(d), device_id_type=MESH)
        return carry

    def greet_q(d, carry):
        pl.semaphore_signal(barrier, inc=1, device_id=qdev(d), device_id_type=MESH)
        return carry

    lax.fori_loop(1, nz, greet_z, 0)
    def greet_o(d, carry):
        pl.semaphore_signal(barrier, inc=1, device_id=odev(d), device_id_type=MESH)
        return carry

    lax.fori_loop(1, nq, greet_q, 0)
    lax.fori_loop(0, nq, greet_o, 0)

    def chain_fill(n, gram, stats):
        p0, p1, d = pack(gram)
        pk[0, :, :] = p0
        pk[1, :, :] = p1
        for h in range(2):
            cs[n, h, 0:gs, :] = pk[h, pl.ds(pl.multiple_of(q * gs, gs), gs), :]
            cs[n, h, gs:gs + 1, :] = d
            for s, row in enumerate(stats):
                cs[n, h, gs + 1 + s:gs + 2 + s, :] = row[:, h * H:(h + 1) * H]
            for s in range(len(stats), STATS - 1):
                cs[n, h, gs + 1 + s:gs + 2 + s, :] = jnp.zeros((1, H), f32)

    def chain_core(n):
        return push_core(cs.at[n, o], ci.at[n])

    def chain_z(n):
        zi[n, z, :, :] = cs[n, c] + ci[n]
        return push_group(nz, zdev, lambda d: zi.at[n, z], zi.at[n, z], zi.at[n, pl.ds(0, nz - 1)])

    def chain_q(n):
        xs[n, c, q, :, :] = jnp.sum(zi[n], axis=0)
        mine = xs.at[n, c, q]
        return (push_group(nq, qdev, lambda d: mine, mine, xs.at[n, c, pl.ds(0, nq - 1)]),
                push_group(nq, odev, lambda d: mine, mine, xs.at[n, c], 0))

    def chain_gram(n):
        return unpack(xs[n, 0, :, 0:gs, :].reshape(H, H), xs[n, 1, :, 0:gs, :].reshape(H, H), xs[n, 0, 0, gs:gs + 1, :])

    def chain_stat(n, qq, s):
        return jnp.concatenate([xs[n, h, qq, gs + 1 + s:gs + 2 + s, :] for h in range(2)], axis=1)

    def add(terms):
        tot = terms[0]
        for term in terms[1:]:
            tot = tot + term
        return tot

    for cp in loads:
        cp.wait()
    f = f_ref[...]
    b = b_ref[...]
    w = w_ref[...]
    shifted = b - 0.5
    wx[k, :, :] = w
    rowp = dot(jnp.ones((8, rj), f32), f, 1, 1)
    colp = jnp.sum(f, axis=0, keepdims=True)
    cq[q, :, :] = colp
    v = dot(jnp.broadcast_to(colp, (8, rj)), shifted)[0:1]
    chain_fill(0, dot(b, b, 0, 0), [v] + [rowp[0:1, i * R:(i + 1) * R] for i in range(ri // R)])
    fa[k, :, :] = f_ref[pl.ds(pl.multiple_of(k * yc, yc), yc), :]

    pl.semaphore_wait(barrier, (nz - 1) + (nq - 1) + nq)

    w_f = push_group(nk, ydev, lambda d: f_ref.at[pl.ds(pl.multiple_of(yto(d) * yc, yc), yc)], fa.at[k], fa.at[pl.ds(0, nk - 1)])
    w_cs = chain_core(0)
    w_w = push_group(nk, ydev, lambda d: wx.at[k], wx.at[k], wx.at[pl.ds(0, nk - 1)])
    w_cs()
    w_z = chain_z(0)
    w_c = push_group(nq, qdev, lambda d: cq.at[q], cq.at[q], cq.at[pl.ds(0, nq - 1)])

    w_w()
    ws = jnp.concatenate([wx[i] for i in range(nk)] + [jnp.zeros((8 - nk, R), f32)], axis=0)
    gram_c = dot(ws, ws, 0, 0)
    w_f()
    g = dot(fa[...].reshape(ri, rj), shifted)
    gw = add([g[i * yc:(i + 1) * yc] * ws[i:i + 1] for i in range(nk)])
    u[0, :, :] = gw[:, 0:H]
    u[1, :, :] = gw[:, H:R]
    w_u = push_core(u.at[o], c_in)
    w_u()
    u[c, :, :] = u[c] + c_in[...]
    z_in[z, :, :] = u[c, pl.ds(pl.multiple_of(z * zc, zc), zc), :]
    w_z3 = push_group(nz, zdev, lambda d: u.at[c, pl.ds(pl.multiple_of(zto(d) * zc, zc), zc)],
                      z_in.at[z], z_in.at[pl.ds(0, nz - 1)])
    w_z()
    w_q, w_b = chain_q(0)
    w_z3()
    tile = ma.at[c, pl.ds(pl.multiple_of(z * zc, zc), zc)]
    tile[...] = jnp.sum(z_in[...], axis=0)
    w_z4 = push_group(nz, zdev, lambda d: tile, tile, ma.at[c, pl.ds(0, yc - zc)])
    w_q()
    w_b()
    h1 = chain_gram(0) * gram_c
    one = eye()
    x1 = inverse(h1)

    w_c()
    zero = jnp.zeros((1, R), f32)
    pad = [jnp.zeros((1, H), f32)] * (8 - nk)
    seg, half = lax.div(k, 2), lax.rem(k, 2)
    coef, totals, cols = [], [], []
    for kk in range(nk):
        grand = add([jnp.sum(chain_stat(0, ee * nk + kk, 1 + i), axis=1, keepdims=True)
                     for ee in range(ne) for i in range(ri // R)])
        coef.append(add([chain_stat(0, ee * nk + kk, 0) for ee in range(ne)]) * ws[kk:kk + 1] / grand)
        totals.append(xs[0, half, e * nk + kk, pl.ds(gs + 2 + seg, 1), :])
        cols.append(add([cq[ee * nk + kk] for ee in range(ne)]) / grand)
    coef = jnp.concatenate(coef + [zero] * (8 - nk), axis=0)
    totals = jnp.concatenate(totals + pad, axis=0)
    week = lax.broadcasted_iota(jnp.int32, (8, 1), 0)
    fix = dot(totals, coef, 0, 0)

    w_z4()
    w_m = push_core(ma.at[c], ma.at[c])
    w_m()
    raw_a = dot(jnp.concatenate([ma[0], ma[1]], axis=1) - fix, x1)

    p0, p1, d = pack(dot(raw_a, raw_a, 0, 0))
    pk[0, :, :] = p0
    pk[1, :, :] = p1
    for i in range(nq):
        gx[i, 0:gs, :] = pk[c, i * gs:(i + 1) * gs, :]
        gx[i, gs:gs + 1, :] = d
    gi[q, :, :] = gx[q]
    w_gi = push_group(nq, qdev, lambda d: gx.at[qto(d)], gi.at[q], gi.at[pl.ds(0, nq - 1)])

    for kk in range(nk):
        only = (week == kk).astype(f32)
        res[:, kk * rj:(kk + 1) * rj] = fa[kk] - dot(totals * only, cols[kk] * only, 0, 0)
    t = dot(res[...], raw_a, 0, 0)
    tw = add([t[i * rj:(i + 1) * rj] * ws[i:i + 1] for i in range(nk)])
    for i in range(nq):
        mos[i, :, :] = tw[i * jc:(i + 1) * jc]
    mi[q, :, :] = mos[q]
    w_mi = push_group(nq, qdev, lambda d: mos.at[qto(d)], mi.at[q], mi.at[pl.ds(0, nq - 1)])
    raw[0, k, :, :] = raw_a[:, 0:H]
    raw[1, k, :, :] = raw_a[:, H:R]

    w_gi()
    gsum = jnp.sum(gi[...], axis=0)
    mine = gag.at[c, pl.ds(pl.multiple_of(q * gs, gs), gs)]
    mine[...] = gsum[0:gs]
    w_ga = push_group(nq, qdev, lambda d: mine, mine, gag.at[c, pl.ds(0, H - gs)])
    w_gc = push_group(nq, odev, lambda d: mine, mine, gag.at[c], 0)
    w_mi()
    mo[q, :, :] = jnp.sum(mi[...], axis=0)
    w_mo = push_group(nq, qdev, lambda d: mo.at[q], mo.at[q], mo.at[pl.ds(0, nq - 1)])
    w_ga()
    w_raw = push_group(nk, ydev, lambda d: raw.at[c, k], raw.at[c, k], raw.at[c, pl.ds(0, nk - 1)])
    w_gc()
    gram_a = unpack(gag[0], gag[1], gsum[gs:gs + 1])

    def unscale(gram, count):
        d = gram * one
        inv_row = 1.0 / jnp.sqrt(jnp.sum(d, axis=0, keepdims=True) / count + eps)
        inv_col = 1.0 / jnp.sqrt(jnp.sum(d, axis=1, keepdims=True) / count + eps)
        return inv_row, gram * inv_row * inv_col

    sa, gram_a = unscale(gram_a, ri * ne)
    h2 = gram_a * gram_c
    x2 = inverse(h2)
    w_mo()
    raw_b = dot(mo[...].reshape(rj, R) * sa, x2)

    chain_fill(1, dot(raw_b, raw_b, 0, 0),
               [jnp.sum(t[i * rj:(i + 1) * rj] * raw_b, axis=0, keepdims=True) for i in range(nk)])
    w_cs = chain_core(1)
    w_cs()
    w_z = chain_z(1)
    w_raw()
    w_rc = push_core(raw.at[c], raw.at[c])
    w_rc()
    a_out[:, 0:H] = raw[0].reshape(ri, H) * sa[:, 0:H]
    a_out[:, H:R] = raw[1].reshape(ri, H) * sa[:, H:R]
    stores[0].start()
    w_z()
    w_q, w_b = chain_q(1)
    w_q()
    w_b()
    sb, gram_b2 = unscale(chain_gram(1), rj * nz * 2)
    b_out[...] = raw_b * sb
    stores[1].start()
    h3 = gram_a * gram_b2
    x3 = inverse(h3)
    scale = sa * sb
    m_c = jnp.concatenate([add([chain_stat(1, qq, kk) for qq in range(nq)]) * scale for kk in range(nk)] + [zero] * (8 - nk), axis=0)
    raw_c = dot(m_c, x3)
    sc = jnp.sqrt(jnp.sum(raw_c * raw_c, axis=0, keepdims=True) / nk + eps)
    c_out[...] = jnp.sum(raw_c * (week == k).astype(f32), axis=0, keepdims=True) / sc
    stores[2].start()

    for fin in pending:
        fin()
    for cp in stores:
        cp.wait()
    assert used[0] == NSEM


NSEM = 22
PARTS = 4


def hand_over(a_in, b_in, c_in, a_out, b_out, c_out, sems):
    rows = a_in.shape[0] // PARTS
    copies = [pltpu.make_async_copy(a_in.at[pl.ds(i * rows, rows)], a_out.at[pl.ds(i * rows, rows)], sems.at[i])
              for i in range(PARTS)]
    copies.append(pltpu.make_async_copy(b_in, b_out, sems.at[PARTS]))
    copies.append(pltpu.make_async_copy(c_in, c_out, sems.at[PARTS + 1]))
    for cp in copies:
        cp.start()
    for cp in copies:
        cp.wait()


def per_device(ne, nz, nk, flows, importer_factor, week_factor):
    ri, rj = flows.shape[1], flows.shape[2]
    nq = ne * nk
    gs = H // nq
    yc = ri // nk
    vm = functools.partial(pltpu.VMEM, dtype=f32)
    shapes = (
        jax.ShapeDtypeStruct((ri, R), f32),
        jax.ShapeDtypeStruct((rj, R), f32),
        jax.ShapeDtypeStruct((1, R), f32),
    )
    outs = pl.pallas_call(
        functools.partial(kernel, ne, nz, nk),
        out_shape=shapes,
        in_specs=[pl.BlockSpec(memory_space=pl.ANY)] * 3,
        out_specs=[pl.BlockSpec(memory_space=pl.ANY)] * 3,
        scratch_shapes=[
            vm((ri, rj)),
            vm((rj, R)),
            vm((1, R)),
            vm((nk, yc, rj)),
            vm((2, yc, H)),
            vm((yc, H)),
            vm((nz, yc // nz, H)),
            vm((2, yc, H)),
            vm((nq, 1, rj)),
            vm((nk, 1, R)),
            vm((2, H, H)),
            vm((2, 2, gs + STATS, H)),
            vm((2, gs + STATS, H)),
            vm((2, nz, gs + STATS, H)),
            vm((2, 2, nq, gs + STATS, H)),
            vm((nq, gs + 1, H)),
            vm((nq, gs + 1, H)),
            vm((2, H, H)),
            vm((nq, rj // nq, R)),
            vm((nq, rj // nq, R)),
            vm((nq, rj // nq, R)),
            vm((yc, nk * rj)),
            vm((2, nk, yc, H)),
            vm((ri, R)),
            vm((rj, R)),
            vm((1, R)),
            pltpu.SemaphoreType.DMA((NSEM,)),
            pltpu.SemaphoreType.DMA((NSEM,)),
            pltpu.SemaphoreType.DMA((6,)),
        ],
        compiler_params=pltpu.CompilerParams(
            collective_id=0, has_side_effects=True, vmem_limit_bytes=60 * 1024 * 1024
        ),
    )(flows, importer_factor, week_factor)
    return pl.pallas_call(
        hand_over,
        out_shape=shapes,
        in_specs=[pl.BlockSpec(memory_space=pl.ANY)] * 3,
        out_specs=[pl.BlockSpec(memory_space=pl.ANY)] * 3,
        scratch_shapes=[pltpu.SemaphoreType.DMA((PARTS + 2,))],
    )(*outs)


def solution(mesh):
    in_specs = (P("wk", "exp", "imp"), P("imp", None), P("wk", None))
    out_specs = (P("exp", None), P("imp", None), P("wk", None))
    fn = functools.partial(per_device, mesh.shape["exp"], mesh.shape["imp"] // 2, mesh.shape["wk"])
    return jax.shard_map(fn, mesh=mesh, in_specs=in_specs, out_specs=out_specs, check_vma=False)
```

```python
import functools

import jax
import jax.numpy as jnp
from jax import lax
from jax.experimental import pallas as pl
from jax.experimental.pallas import tpu as pltpu
from jax.sharding import PartitionSpec as P

ridge = 0.2
eps = 1e-06
hp = lax.Precision.HIGHEST
f32 = jnp.float32
bf16 = jnp.bfloat16
R = 256
H = 128
MESH = pl.DeviceIdType.MESH
STATS = 5
STEPS = 7


def dot(a, b, ca=1, cb=0):
    return lax.dot_general(a, b, (((ca,), (cb,)), ((), ())), precision=hp, preferred_element_type=f32)


def split(a):
    hi = a.astype(bf16)
    return hi, (a - hi.astype(f32)).astype(bf16)


def dot3(a, b):
    ah, al = a
    bh, bl = b
    d = functools.partial(jnp.dot, preferred_element_type=f32)
    return d(ah, bh) + (d(ah, bl) + d(al, bh))


def eye():
    return (lax.broadcasted_iota(jnp.int32, (R, R), 0) == lax.broadcasted_iota(jnp.int32, (R, R), 1)).astype(f32)


def inverse(h):
    one = eye()
    lam = ridge * jnp.sum(h * one) / R
    v = h + lam * one
    top = 1.0 + R / ridge
    alpha = 2.0 / (lam * (1.0 + top))
    delta = (top - 1.0) / (top + 1.0)
    e = one - alpha * v
    for step in range(STEPS):
        c = 2.0 / (2.0 - delta * delta)
        delta = delta * delta / (2.0 - delta * delta)
        se = split(e)
        x = (c * alpha) * (one + e) if step == 0 else c * (x + dot3(split(x), se))
        if step < STEPS - 1:
            e = c * dot3(se, se) + (1.0 - c) * one
    r = one - dot(v, x)
    return x + dot3(split(x), split(r))


def triangle():
    r = lax.broadcasted_iota(jnp.int32, (H, H), 0)
    c = lax.broadcasted_iota(jnp.int32, (H, H), 1)
    return r, c


def pack(g):
    r, c = triangle()
    g11 = g[H:, H:]
    return jnp.where(r <= c, g[:H, :H], g11), g[:H, H:], jnp.sum(jnp.where(r == c, g11, 0.0), axis=0, keepdims=True)


def unpack(p0, p1, d):
    r, c = triangle()
    g00 = jnp.where(r <= c, p0, 0.0) + jnp.where(r < c, p0, 0.0).T
    low = jnp.where(r > c, p0, 0.0)
    g11 = low + low.T + jnp.where(r == c, d, 0.0)
    return jnp.concatenate(
        [jnp.concatenate([g00, p1], axis=1), jnp.concatenate([p1.T, g11], axis=1)], axis=0)


def kernel(ne, nz, nk, f_hbm, b_hbm, w_hbm, a_hbm, b_out_hbm, c_hbm,
           f_ref, b_ref, w_ref, fa, u, c_in, z_in, ma, cq, wx,
           pk, cs, ci, zi, xs, gi, gx, gag, mi, mo, mos, res, raw, a_out, b_out, c_out,
           ssem, rsem, lsem):
    e = lax.axis_index("exp")
    p = lax.axis_index("imp")
    k = lax.axis_index("wk")
    z = lax.div(p, 2)
    c = lax.rem(p, 2)
    o = 1 - c
    nq = ne * nk
    q = e * nk + k
    ri, rj = f_ref.shape
    yc = ri // nk
    zc = yc // nz
    jc = rj // nq
    gs = H // nq
    used = [0]
    pending = []

    loads = [pltpu.make_async_copy(f_hbm.at[0], f_ref, lsem.at[0]),
             pltpu.make_async_copy(b_hbm, b_ref, lsem.at[1]),
             pltpu.make_async_copy(w_hbm, w_ref, lsem.at[2])]
    for cp in loads:
        cp.start()
    stores = [pltpu.make_async_copy(src, dst, lsem.at[3 + i])
              for i, (src, dst) in enumerate([(a_out, a_hbm), (b_out, b_out_hbm), (c_out, c_hbm)])]

    def take():
        used[0] += 1
        return used[0] - 1

    def remote(src, dst, s, dev):
        return pltpu.make_async_remote_copy(
            src_ref=src, dst_ref=dst, send_sem=ssem.at[s], recv_sem=rsem.at[s],
            device_id=dev, device_id_type=MESH)

    core_dev = {"imp": z * 2 + o}

    def push_core(src, dst):
        cp = remote(src, dst, take(), core_dev)
        cp.start()
        pending.append(cp.wait_send)
        return cp.wait_recv

    def push_group(n, dev, src, dst, every, first=1):
        s = take()

        def go(d, carry):
            remote(src(d), dst, s, dev(d)).start()
            return carry

        lax.fori_loop(first, n, go, 0)
        cp = remote(every, every, s, dev(1))
        pending.append(cp.wait_send)
        return cp.wait_recv

    def zto(d):
        return lax.rem(z + d, nz)

    def zdev(d):
        return {"imp": zto(d) * 2 + c}

    def yto(d):
        return lax.rem(k + d, nk)

    def ydev(d):
        return {"wk": yto(d)}

    def qto(d):
        return lax.rem(q + d, nq)

    def qdev(d):
        return {"exp": lax.div(qto(d), nk), "wk": lax.rem(qto(d), nk)}

    def odev(d):
        return {"exp": lax.div(qto(d), nk), "wk": lax.rem(qto(d), nk), "imp": z * 2 + o}

    barrier = pltpu.get_barrier_semaphore()
    def greet_z(d, carry):
        pl.semaphore_signal(barrier, inc=1, device_id=zdev(d), device_id_type=MESH)
        return carry

    def greet_q(d, carry):
        pl.semaphore_signal(barrier, inc=1, device_id=qdev(d), device_id_type=MESH)
        return carry

    lax.fori_loop(1, nz, greet_z, 0)
    def greet_o(d, carry):
        pl.semaphore_signal(barrier, inc=1, device_id=odev(d), device_id_type=MESH)
        return carry

    lax.fori_loop(1, nq, greet_q, 0)
    lax.fori_loop(0, nq, greet_o, 0)

    def chain_fill(n, gram, stats):
        p0, p1, d = pack(gram)
        pk[0, :, :] = p0
        pk[1, :, :] = p1
        for h in range(2):
            cs[n, h, 0:gs, :] = pk[h, pl.ds(pl.multiple_of(q * gs, gs), gs), :]
            cs[n, h, gs:gs + 1, :] = d
            for s, row in enumerate(stats):
                cs[n, h, gs + 1 + s:gs + 2 + s, :] = row[:, h * H:(h + 1) * H]
            for s in range(len(stats), STATS - 1):
                cs[n, h, gs + 1 + s:gs + 2 + s, :] = jnp.zeros((1, H), f32)

    def chain_core(n):
        return push_core(cs.at[n, o], ci.at[n])

    def chain_z(n):
        zi[n, z, :, :] = cs[n, c] + ci[n]
        return push_group(nz, zdev, lambda d: zi.at[n, z], zi.at[n, z], zi.at[n, pl.ds(0, nz - 1)])

    def chain_q(n):
        xs[n, c, q, :, :] = jnp.sum(zi[n], axis=0)
        mine = xs.at[n, c, q]
        return (push_group(nq, qdev, lambda d: mine, mine, xs.at[n, c, pl.ds(0, nq - 1)]),
                push_group(nq, odev, lambda d: mine, mine, xs.at[n, c], 0))

    def chain_gram(n):
        return unpack(xs[n, 0, :, 0:gs, :].reshape(H, H), xs[n, 1, :, 0:gs, :].reshape(H, H), xs[n, 0, 0, gs:gs + 1, :])

    def chain_stat(n, qq, s):
        return jnp.concatenate([xs[n, h, qq, gs + 1 + s:gs + 2 + s, :] for h in range(2)], axis=1)

    def add(terms):
        tot = terms[0]
        for term in terms[1:]:
            tot = tot + term
        return tot

    for cp in loads:
        cp.wait()
    f = f_ref[...]
    b = b_ref[...]
    w = w_ref[...]
    shifted = b - 0.5
    wx[k, :, :] = w
    rowp = dot(jnp.ones((8, rj), f32), f, 1, 1)
    colp = jnp.sum(f, axis=0, keepdims=True)
    cq[q, :, :] = colp
    v = dot(jnp.broadcast_to(colp, (8, rj)), shifted)[0:1]
    chain_fill(0, dot(b, b, 0, 0), [v] + [rowp[0:1, i * R:(i + 1) * R] for i in range(ri // R)])
    fa[k, :, :] = f_ref[pl.ds(pl.multiple_of(k * yc, yc), yc), :]

    pl.semaphore_wait(barrier, (nz - 1) + (nq - 1) + nq)

    w_f = push_group(nk, ydev, lambda d: f_ref.at[pl.ds(pl.multiple_of(yto(d) * yc, yc), yc)], fa.at[k], fa.at[pl.ds(0, nk - 1)])
    w_cs = chain_core(0)
    w_w = push_group(nk, ydev, lambda d: wx.at[k], wx.at[k], wx.at[pl.ds(0, nk - 1)])
    w_cs()
    w_z = chain_z(0)
    w_c = push_group(nq, qdev, lambda d: cq.at[q], cq.at[q], cq.at[pl.ds(0, nq - 1)])

    w_w()
    ws = jnp.concatenate([wx[i] for i in range(nk)] + [jnp.zeros((8 - nk, R), f32)], axis=0)
    gram_c = dot(ws, ws, 0, 0)
    w_f()
    g = dot(fa[...].reshape(ri, rj), shifted)
    gw = add([g[i * yc:(i + 1) * yc] * ws[i:i + 1] for i in range(nk)])
    u[0, :, :] = gw[:, 0:H]
    u[1, :, :] = gw[:, H:R]
    w_u = push_core(u.at[o], c_in)
    w_u()
    u[c, :, :] = u[c] + c_in[...]
    z_in[z, :, :] = u[c, pl.ds(pl.multiple_of(z * zc, zc), zc), :]
    w_z3 = push_group(nz, zdev, lambda d: u.at[c, pl.ds(pl.multiple_of(zto(d) * zc, zc), zc)],
                      z_in.at[z], z_in.at[pl.ds(0, nz - 1)])
    w_z()
    w_q, w_b = chain_q(0)
    w_z3()
    tile = ma.at[c, pl.ds(pl.multiple_of(z * zc, zc), zc)]
    tile[...] = jnp.sum(z_in[...], axis=0)
    w_z4 = push_group(nz, zdev, lambda d: tile, tile, ma.at[c, pl.ds(0, yc - zc)])
    w_q()
    w_b()
    h1 = chain_gram(0) * gram_c
    one = eye()
    x1 = inverse(h1)

    w_c()
    zero = jnp.zeros((1, R), f32)
    pad = [jnp.zeros((1, H), f32)] * (8 - nk)
    seg, half = lax.div(k, 2), lax.rem(k, 2)
    coef, totals, cols = [], [], []
    for kk in range(nk):
        grand = add([jnp.sum(chain_stat(0, ee * nk + kk, 1 + i), axis=1, keepdims=True)
                     for ee in range(ne) for i in range(ri // R)])
        coef.append(add([chain_stat(0, ee * nk + kk, 0) for ee in range(ne)]) * ws[kk:kk + 1] / grand)
        totals.append(xs[0, half, e * nk + kk, pl.ds(gs + 2 + seg, 1), :])
        cols.append(add([cq[ee * nk + kk] for ee in range(ne)]) / grand)
    coef = jnp.concatenate(coef + [zero] * (8 - nk), axis=0)
    totals = jnp.concatenate(totals + pad, axis=0)
    week = lax.broadcasted_iota(jnp.int32, (8, 1), 0)
    fix = dot(totals, coef, 0, 0)

    w_z4()
    w_m = push_core(ma.at[c], ma.at[c])
    w_m()
    raw_a = dot(jnp.concatenate([ma[0], ma[1]], axis=1) - fix, x1)

    p0, p1, d = pack(dot(raw_a, raw_a, 0, 0))
    pk[0, :, :] = p0
    pk[1, :, :] = p1
    for i in range(nq):
        gx[i, 0:gs, :] = pk[c, i * gs:(i + 1) * gs, :]
        gx[i, gs:gs + 1, :] = d
    gi[q, :, :] = gx[q]
    w_gi = push_group(nq, qdev, lambda d: gx.at[qto(d)], gi.at[q], gi.at[pl.ds(0, nq - 1)])

    for kk in range(nk):
        only = (week == kk).astype(f32)
        res[:, kk * rj:(kk + 1) * rj] = fa[kk] - dot(totals * only, cols[kk] * only, 0, 0)
    t = dot(res[...], raw_a, 0, 0)
    tw = add([t[i * rj:(i + 1) * rj] * ws[i:i + 1] for i in range(nk)])
    for i in range(nq):
        mos[i, :, :] = tw[i * jc:(i + 1) * jc]
    mi[q, :, :] = mos[q]
    w_mi = push_group(nq, qdev, lambda d: mos.at[qto(d)], mi.at[q], mi.at[pl.ds(0, nq - 1)])
    raw[0, k, :, :] = raw_a[:, 0:H]
    raw[1, k, :, :] = raw_a[:, H:R]

    w_gi()
    gsum = jnp.sum(gi[...], axis=0)
    mine = gag.at[c, pl.ds(pl.multiple_of(q * gs, gs), gs)]
    mine[...] = gsum[0:gs]
    w_ga = push_group(nq, qdev, lambda d: mine, mine, gag.at[c, pl.ds(0, H - gs)])
    w_gc = push_group(nq, odev, lambda d: mine, mine, gag.at[c], 0)
    w_mi()
    mo[q, :, :] = jnp.sum(mi[...], axis=0)
    w_mo = push_group(nq, qdev, lambda d: mo.at[q], mo.at[q], mo.at[pl.ds(0, nq - 1)])
    w_ga()
    w_raw = push_group(nk, ydev, lambda d: raw.at[c, k], raw.at[c, k], raw.at[c, pl.ds(0, nk - 1)])
    w_gc()
    gram_a = unpack(gag[0], gag[1], gsum[gs:gs + 1])

    def unscale(gram, count):
        d = gram * one
        inv_row = 1.0 / jnp.sqrt(jnp.sum(d, axis=0, keepdims=True) / count + eps)
        inv_col = 1.0 / jnp.sqrt(jnp.sum(d, axis=1, keepdims=True) / count + eps)
        return inv_row, gram * inv_row * inv_col

    sa, gram_a = unscale(gram_a, ri * ne)
    h2 = gram_a * gram_c
    x2 = inverse(h2)
    w_mo()
    raw_b = dot(mo[...].reshape(rj, R) * sa, x2)

    chain_fill(1, dot(raw_b, raw_b, 0, 0),
               [jnp.sum(t[i * rj:(i + 1) * rj] * raw_b, axis=0, keepdims=True) for i in range(nk)])
    w_cs = chain_core(1)
    w_cs()
    w_z = chain_z(1)
    w_raw()
    w_rc = push_core(raw.at[c], raw.at[c])
    w_rc()
    a_out[:, 0:H] = raw[0].reshape(ri, H) * sa[:, 0:H]
    a_out[:, H:R] = raw[1].reshape(ri, H) * sa[:, H:R]
    stores[0].start()
    w_z()
    w_q, w_b = chain_q(1)
    w_q()
    w_b()
    sb, gram_b2 = unscale(chain_gram(1), rj * nz * 2)
    b_out[...] = raw_b * sb
    stores[1].start()
    h3 = gram_a * gram_b2
    x3 = inverse(h3)
    scale = sa * sb
    m_c = jnp.concatenate([add([chain_stat(1, qq, kk) for qq in range(nq)]) * scale for kk in range(nk)] + [zero] * (8 - nk), axis=0)
    raw_c = dot(m_c, x3)
    sc = jnp.sqrt(jnp.sum(raw_c * raw_c, axis=0, keepdims=True) / nk + eps)
    c_out[...] = jnp.sum(raw_c * (week == k).astype(f32), axis=0, keepdims=True) / sc
    stores[2].start()

    for fin in pending:
        fin()
    for cp in stores:
        cp.wait()
    assert used[0] == NSEM


NSEM = 22
PARTS = 4


def hand_over(a_in, b_in, c_in, a_out, b_out, c_out, a, b, c, load, store):
    rows = a_in.shape[0] // PARTS
    steps = [(x_in.at[pl.ds(i * n, n)], x.at[pl.ds(i * n, n)], x_out.at[pl.ds(i * n, n)])
             for x_in, x, x_out, n, parts in ((a_in, a, a_out, rows, PARTS), (b_in, b, b_out, b_in.shape[0], 1))
             for i in range(parts)] + [(c_in, c, c_out)]
    loads = [pltpu.make_async_copy(src, mid, load.at[i]) for i, (src, mid, dst) in enumerate(steps)]
    stores = [pltpu.make_async_copy(mid, dst, store.at[i]) for i, (src, mid, dst) in enumerate(steps)]
    for cp in loads:
        cp.start()
    for first, then in zip(loads, stores):
        first.wait()
        then.start()
    for cp in stores:
        cp.wait()


def per_device(ne, nz, nk, flows, importer_factor, week_factor):
    ri, rj = flows.shape[1], flows.shape[2]
    nq = ne * nk
    gs = H // nq
    yc = ri // nk
    vm = functools.partial(pltpu.VMEM, dtype=f32)
    shapes = (
        jax.ShapeDtypeStruct((ri, R), f32),
        jax.ShapeDtypeStruct((rj, R), f32),
        jax.ShapeDtypeStruct((1, R), f32),
    )
    outs = pl.pallas_call(
        functools.partial(kernel, ne, nz, nk),
        out_shape=shapes,
        in_specs=[pl.BlockSpec(memory_space=pl.ANY)] * 3,
        out_specs=[pl.BlockSpec(memory_space=pl.ANY)] * 3,
        scratch_shapes=[
            vm((ri, rj)),
            vm((rj, R)),
            vm((1, R)),
            vm((nk, yc, rj)),
            vm((2, yc, H)),
            vm((yc, H)),
            vm((nz, yc // nz, H)),
            vm((2, yc, H)),
            vm((nq, 1, rj)),
            vm((nk, 1, R)),
            vm((2, H, H)),
            vm((2, 2, gs + STATS, H)),
            vm((2, gs + STATS, H)),
            vm((2, nz, gs + STATS, H)),
            vm((2, 2, nq, gs + STATS, H)),
            vm((nq, gs + 1, H)),
            vm((nq, gs + 1, H)),
            vm((2, H, H)),
            vm((nq, rj // nq, R)),
            vm((nq, rj // nq, R)),
            vm((nq, rj // nq, R)),
            vm((yc, nk * rj)),
            vm((2, nk, yc, H)),
            vm((ri, R)),
            vm((rj, R)),
            vm((1, R)),
            pltpu.SemaphoreType.DMA((NSEM,)),
            pltpu.SemaphoreType.DMA((NSEM,)),
            pltpu.SemaphoreType.DMA((6,)),
        ],
        compiler_params=pltpu.CompilerParams(
            collective_id=0, has_side_effects=True, vmem_limit_bytes=60 * 1024 * 1024
        ),
    )(flows, importer_factor, week_factor)
    return pl.pallas_call(
        hand_over,
        out_shape=shapes,
        in_specs=[pl.BlockSpec(memory_space=pl.ANY)] * 3,
        out_specs=[pl.BlockSpec(memory_space=pl.ANY)] * 3,
        scratch_shapes=[vm((ri, R)), vm((rj, R)), vm((1, R))] + [pltpu.SemaphoreType.DMA((PARTS + 2,))] * 2,
    )(*outs)


def solution(mesh):
    in_specs = (P("wk", "exp", "imp"), P("imp", None), P("wk", None))
    out_specs = (P("exp", None), P("imp", None), P("wk", None))
    fn = functools.partial(per_device, mesh.shape["exp"], mesh.shape["imp"] // 2, mesh.shape["wk"])
    return jax.shard_map(fn, mesh=mesh, in_specs=in_specs, out_specs=out_specs, check_vma=False)
```

```python
import functools

import jax
import jax.numpy as jnp
from jax import lax
from jax.experimental import pallas as pl
from jax.experimental.pallas import tpu as pltpu
from jax.sharding import PartitionSpec as P

ridge = 0.2
eps = 1e-06
hp = lax.Precision.HIGHEST
f32 = jnp.float32
bf16 = jnp.bfloat16
R = 256
H = 128
MESH = pl.DeviceIdType.MESH
STATS = 5
STEPS = 7


def dot(a, b, ca=1, cb=0):
    return lax.dot_general(a, b, (((ca,), (cb,)), ((), ())), precision=hp, preferred_element_type=f32)


def split(a):
    hi = a.astype(bf16)
    return hi, (a - hi.astype(f32)).astype(bf16)


def dot3(a, b):
    ah, al = a
    bh, bl = b
    d = functools.partial(jnp.dot, preferred_element_type=f32)
    return d(ah, bh) + (d(ah, bl) + d(al, bh))


def eye():
    return (lax.broadcasted_iota(jnp.int32, (R, R), 0) == lax.broadcasted_iota(jnp.int32, (R, R), 1)).astype(f32)


def nearly(h):
    one = eye()
    lam = ridge * jnp.sum(h * one) / R
    v = h + lam * one
    top = 1.0 + R / ridge
    alpha = 2.0 / (lam * (1.0 + top))
    delta = (top - 1.0) / (top + 1.0)
    e = one - alpha * v
    for step in range(STEPS):
        c = 2.0 / (2.0 - delta * delta)
        delta = delta * delta / (2.0 - delta * delta)
        se = split(e)
        x = (c * alpha) * (one + e) if step == 0 else c * (x + dot3(split(x), se))
        if step < STEPS - 1:
            e = c * dot3(se, se) + (1.0 - c) * one
    return v, x


def inverse(h):
    v, x = nearly(h)
    return x + dot3(split(x), split(eye() - dot(v, x)))


def solve(m, h):
    v, x = nearly(h)
    x = split(x)
    y = dot3(split(m), x)
    return y + dot3(split(m - dot(y, v)), x)


def triangle():
    r = lax.broadcasted_iota(jnp.int32, (H, H), 0)
    c = lax.broadcasted_iota(jnp.int32, (H, H), 1)
    return r, c


def pack(g):
    r, c = triangle()
    g11 = g[H:, H:]
    return jnp.where(r <= c, g[:H, :H], g11), g[:H, H:], jnp.sum(jnp.where(r == c, g11, 0.0), axis=0, keepdims=True)


def unpack(p0, p1, d):
    r, c = triangle()
    g00 = jnp.where(r <= c, p0, 0.0) + jnp.where(r < c, p0, 0.0).T
    low = jnp.where(r > c, p0, 0.0)
    g11 = low + low.T + jnp.where(r == c, d, 0.0)
    return jnp.concatenate(
        [jnp.concatenate([g00, p1], axis=1), jnp.concatenate([p1.T, g11], axis=1)], axis=0)


def kernel(ne, nz, nk, f_hbm, b_hbm, w_hbm, a_hbm, b_out_hbm, c_hbm,
           f_ref, b_ref, w_ref, fa, u, z_in, ma, cq, wx,
           pk, cs, ci, zi, xs, gi, gx, gag, mi, mo, mos, res, raw, a_out, b_out, c_out,
           ssem, rsem, lsem):
    e = lax.axis_index("exp")
    p = lax.axis_index("imp")
    k = lax.axis_index("wk")
    z = lax.div(p, 2)
    c = lax.rem(p, 2)
    o = 1 - c
    nq = ne * nk
    q = e * nk + k
    ri, rj = f_ref.shape
    yc = ri // nk
    zc = yc // nz
    jc = rj // nq
    gs = H // nq
    used = [0]
    pending = []

    loads = [pltpu.make_async_copy(f_hbm.at[0], f_ref, lsem.at[0]),
             pltpu.make_async_copy(b_hbm, b_ref, lsem.at[1]),
             pltpu.make_async_copy(w_hbm, w_ref, lsem.at[2])]
    for cp in loads:
        cp.start()
    stores = [pltpu.make_async_copy(src, dst, lsem.at[3 + i])
              for i, (src, dst) in enumerate([(a_out, a_hbm), (b_out, b_out_hbm), (c_out, c_hbm)])]

    def take():
        used[0] += 1
        return used[0] - 1

    def remote(src, dst, s, dev):
        return pltpu.make_async_remote_copy(
            src_ref=src, dst_ref=dst, send_sem=ssem.at[s], recv_sem=rsem.at[s],
            device_id=dev, device_id_type=MESH)

    core_dev = {"imp": z * 2 + o}

    def push_core(src, dst):
        cp = remote(src, dst, take(), core_dev)
        cp.start()
        pending.append(cp.wait_send)
        return cp.wait_recv

    def push_group(n, dev, src, dst, every, first=1):
        s = take()

        def go(i, carry):
            d = far(i, n)
            remote(src(d), dst, s, dev(d)).start()
            return carry

        lax.fori_loop(0, n - first, go, 0)
        cp = remote(every, every, s, dev(1))
        pending.append(cp.wait_send)
        return cp.wait_recv

    def push_both(n, dev, dev_o, src, src_o, dst, every, every_o):
        s, s_o = take(), take()

        def go(i, carry):
            d = far(i, n)
            remote(src(d), dst, s, dev(d)).start()
            remote(src_o(d), dst, s_o, dev_o(d)).start()
            return carry

        lax.fori_loop(0, n - 1, go, 0)
        remote(src_o(0), dst, s_o, dev_o(0)).start()
        cp = remote(every, every, s, dev(1))
        cp_o = remote(every_o, every_o, s_o, dev_o(0))
        pending.extend([cp.wait_send, cp_o.wait_send])

        def wait():
            cp.wait_recv()
            cp_o.wait_recv()

        return wait

    def far(i, n):
        h = lax.div(i + 1, 2)
        return lax.rem(n // 2 + jnp.where(lax.rem(i, 2) == 1, h, -h), n)

    def zto(d):
        return lax.rem(z + d, nz)

    def zdev(d):
        return {"imp": zto(d) * 2 + c}

    def zodev(d):
        return {"imp": zto(d) * 2 + o}

    def yto(d):
        return lax.rem(k + d, nk)

    def ydev(d):
        return {"wk": yto(d)}

    def qto(d):
        return lax.rem(q + d, nq)

    def qdev(d):
        return {"exp": lax.div(qto(d), nk), "wk": lax.rem(qto(d), nk)}

    def odev(d):
        return {"exp": lax.div(qto(d), nk), "wk": lax.rem(qto(d), nk), "imp": z * 2 + o}

    barrier = pltpu.get_barrier_semaphore()
    def greet(n, first, dev):
        def one_device(i, carry):
            pl.semaphore_signal(barrier, inc=1, device_id=dev(far(i, n)), device_id_type=MESH)
            return carry

        lax.fori_loop(0, n - first, one_device, 0)

    greet(nz, 1, zdev)
    greet(nz, 0, zodev)
    greet(nq, 1, qdev)
    greet(nq, 1, odev)

    def chain_fill(n, gram, stats):
        p0, p1, d = pack(gram)
        pk[0, :, :] = p0
        pk[1, :, :] = p1
        for h in range(2):
            cs[n, h, 0:gs, :] = pk[h, pl.ds(pl.multiple_of(q * gs, gs), gs), :]
            cs[n, h, gs:gs + 1, :] = d
            for s, row in enumerate(stats):
                cs[n, h, gs + 1 + s:gs + 2 + s, :] = row[:, h * H:(h + 1) * H]
            for s in range(len(stats), STATS - 1):
                cs[n, h, gs + 1 + s:gs + 2 + s, :] = jnp.zeros((1, H), f32)

    def chain_core(n):
        return push_core(cs.at[n, o], ci.at[n])

    def chain_z(n):
        zi[n, z, :, :] = cs[n, c] + ci[n]
        return push_group(nz, zdev, lambda d: zi.at[n, z], zi.at[n, z], zi.at[n, pl.ds(0, nz - 1)])

    def chain_q(n):
        xs[n, c, q, :, :] = jnp.sum(zi[n], axis=0)
        mine = xs.at[n, c, q]
        return push_both(nq, qdev, odev, lambda d: mine, lambda d: mine, mine, xs.at[n, c, pl.ds(0, nq - 1)], xs.at[n, c])

    def chain_gram(n):
        return unpack(xs[n, 0, :, 0:gs, :].reshape(H, H), xs[n, 1, :, 0:gs, :].reshape(H, H), xs[n, 0, 0, gs:gs + 1, :])

    def chain_stat(n, qq, s):
        return jnp.concatenate([xs[n, h, qq, gs + 1 + s:gs + 2 + s, :] for h in range(2)], axis=1)

    def add(terms):
        tot = terms[0]
        for term in terms[1:]:
            tot = tot + term
        return tot

    for cp in loads:
        cp.wait()
    f = f_ref[...]
    b = b_ref[...]
    w = w_ref[...]
    shifted = b - 0.5
    wx[k, :, :] = w
    rowp = dot(jnp.ones((8, rj), f32), f, 1, 1)
    colp = jnp.sum(f, axis=0, keepdims=True)
    cq[q, :, :] = colp
    v = dot(jnp.broadcast_to(colp, (8, rj)), shifted)[0:1]
    chain_fill(0, dot(b, b, 0, 0), [v] + [rowp[0:1, i * R:(i + 1) * R] for i in range(ri // R)])
    fa[k, :, :] = f_ref[pl.ds(pl.multiple_of(k * yc, yc), yc), :]

    pl.semaphore_wait(barrier, (nz - 1) + nz + 2 * (nq - 1))

    w_f = push_group(nk, ydev, lambda d: f_ref.at[pl.ds(pl.multiple_of(yto(d) * yc, yc), yc)], fa.at[k], fa.at[pl.ds(0, nk - 1)])
    w_cs = chain_core(0)
    w_w = push_group(nk, ydev, lambda d: wx.at[k], wx.at[k], wx.at[pl.ds(0, nk - 1)])
    w_cs()
    w_z = chain_z(0)
    w_c = push_group(nq, qdev, lambda d: cq.at[q], cq.at[q], cq.at[pl.ds(0, nq - 1)])

    w_w()
    ws = jnp.concatenate([wx[i] for i in range(nk)] + [jnp.zeros((8 - nk, R), f32)], axis=0)
    gram_c = dot(ws, ws, 0, 0)
    w_f()
    g = dot(fa[...].reshape(ri, rj), shifted)
    gw = add([g[i * yc:(i + 1) * yc] * ws[i:i + 1] for i in range(nk)])
    u[0, :, :] = gw[:, 0:H]
    u[1, :, :] = gw[:, H:R]
    def cut(h, zz):
        return u.at[h, pl.ds(pl.multiple_of(zz * zc, zc), zc)]

    z_in[p, :, :] = cut(c, z)[...]
    w_z3 = push_both(nz, zdev, zodev, lambda d: cut(c, zto(d)), lambda d: cut(o, zto(d)), z_in.at[p],
                     z_in.at[pl.ds(0, nz - 1)], z_in.at[pl.ds(0, nz)])
    w_z()
    w_q = chain_q(0)
    w_z3()
    tile = ma.at[c, pl.ds(pl.multiple_of(z * zc, zc), zc)]
    tile[...] = jnp.sum(z_in[...], axis=0)
    w_z4 = push_both(nz, zdev, zodev, lambda d: tile, lambda d: tile, tile, ma.at[c, pl.ds(0, yc - zc)], ma.at[c])
    w_q()
    h1 = chain_gram(0) * gram_c
    one = eye()
    x1 = inverse(h1)

    w_c()
    zero = jnp.zeros((1, R), f32)
    pad = [jnp.zeros((1, H), f32)] * (8 - nk)
    seg, half = lax.div(k, 2), lax.rem(k, 2)
    coef, totals, cols = [], [], []
    for kk in range(nk):
        grand = add([jnp.sum(chain_stat(0, ee * nk + kk, 1 + i), axis=1, keepdims=True)
                     for ee in range(ne) for i in range(ri // R)])
        coef.append(add([chain_stat(0, ee * nk + kk, 0) for ee in range(ne)]) * ws[kk:kk + 1] / grand)
        totals.append(xs[0, half, e * nk + kk, pl.ds(gs + 2 + seg, 1), :])
        cols.append(add([cq[ee * nk + kk] for ee in range(ne)]) / grand)
    coef = jnp.concatenate(coef + [zero] * (8 - nk), axis=0)
    totals = jnp.concatenate(totals + pad, axis=0)
    week = lax.broadcasted_iota(jnp.int32, (8, 1), 0)
    fix = dot(totals, coef, 0, 0)

    w_z4()
    raw_a = dot(jnp.concatenate([ma[0], ma[1]], axis=1) - fix, x1)

    p0, p1, d = pack(dot(raw_a, raw_a, 0, 0))
    pk[0, :, :] = p0
    pk[1, :, :] = p1
    for i in range(nq):
        gx[i, 0:gs, :] = pk[c, i * gs:(i + 1) * gs, :]
        gx[i, gs:gs + 1, :] = d
    gi[q, :, :] = gx[q]
    w_gi = push_group(nq, qdev, lambda d: gx.at[qto(d)], gi.at[q], gi.at[pl.ds(0, nq - 1)])

    for kk in range(nk):
        only = (week == kk).astype(f32)
        res[:, kk * rj:(kk + 1) * rj] = fa[kk] - dot(totals * only, cols[kk] * only, 0, 0)
    t = dot(res[...], raw_a, 0, 0)
    tw = add([t[i * rj:(i + 1) * rj] * ws[i:i + 1] for i in range(nk)])
    for i in range(nq):
        mos[i, :, :] = tw[i * jc:(i + 1) * jc]
    mi[q, :, :] = mos[q]
    w_mi = push_group(nq, qdev, lambda d: mos.at[qto(d)], mi.at[q], mi.at[pl.ds(0, nq - 1)])
    raw[0, k, :, :] = raw_a[:, 0:H]
    raw[1, k, :, :] = raw_a[:, H:R]

    w_gi()
    gsum = jnp.sum(gi[...], axis=0)
    mine = gag.at[c, pl.ds(pl.multiple_of(q * gs, gs), gs)]
    mine[...] = gsum[0:gs]
    w_ga = push_both(nq, qdev, odev, lambda d: mine, lambda d: mine, mine, gag.at[c, pl.ds(0, H - gs)], gag.at[c])
    w_mi()
    mo[q, :, :] = jnp.sum(mi[...], axis=0)
    w_mo = push_group(nq, qdev, lambda d: mo.at[q], mo.at[q], mo.at[pl.ds(0, nq - 1)])
    w_ga()
    w_raw = push_group(nk, ydev, lambda d: raw.at[c, k], raw.at[c, k], raw.at[c, pl.ds(0, nk - 1)])
    gram_a = unpack(gag[0], gag[1], gsum[gs:gs + 1])

    def unscale(gram, count):
        d = gram * one
        inv_row = 1.0 / jnp.sqrt(jnp.sum(d, axis=0, keepdims=True) / count + eps)
        inv_col = 1.0 / jnp.sqrt(jnp.sum(d, axis=1, keepdims=True) / count + eps)
        return inv_row, gram * inv_row * inv_col

    sa, gram_a = unscale(gram_a, ri * ne)
    h2 = gram_a * gram_c
    w_mo()
    raw_b = solve(mo[...].reshape(rj, R) * sa, h2)

    chain_fill(1, dot(raw_b, raw_b, 0, 0),
               [jnp.sum(t[i * rj:(i + 1) * rj] * raw_b, axis=0, keepdims=True) for i in range(nk)])
    w_cs = chain_core(1)
    w_cs()
    w_z = chain_z(1)
    w_raw()
    w_rc = push_core(raw.at[c], raw.at[c])
    w_rc()
    a_out[:, 0:H] = raw[0].reshape(ri, H) * sa[:, 0:H]
    a_out[:, H:R] = raw[1].reshape(ri, H) * sa[:, H:R]
    stores[0].start()
    w_z()
    w_q = chain_q(1)
    w_q()
    sb, gram_b2 = unscale(chain_gram(1), rj * nz * 2)
    b_out[...] = raw_b * sb
    stores[1].start()
    h3 = gram_a * gram_b2
    scale = sa * sb
    m_c = jnp.concatenate([add([chain_stat(1, qq, kk) for qq in range(nq)]) * scale for kk in range(nk)] + [zero] * (8 - nk), axis=0)
    raw_c = solve(m_c, h3)
    sc = jnp.sqrt(jnp.sum(raw_c * raw_c, axis=0, keepdims=True) / nk + eps)
    c_out[...] = jnp.sum(raw_c * (week == k).astype(f32), axis=0, keepdims=True) / sc
    stores[2].start()

    for fin in pending:
        fin()
    for cp in stores:
        cp.wait()
    assert used[0] == NSEM


NSEM = 22
PARTS = 4


def hand_over(a_in, b_in, c_in, a_out, b_out, c_out, a, b, c, load, store):
    rows = a_in.shape[0] // PARTS
    steps = [(x_in.at[pl.ds(i * n, n)], x.at[pl.ds(i * n, n)], x_out.at[pl.ds(i * n, n)])
             for x_in, x, x_out, n, parts in ((a_in, a, a_out, rows, PARTS), (b_in, b, b_out, b_in.shape[0], 1))
             for i in range(parts)] + [(c_in, c, c_out)]
    loads = [pltpu.make_async_copy(src, mid, load.at[i]) for i, (src, mid, dst) in enumerate(steps)]
    stores = [pltpu.make_async_copy(mid, dst, store.at[i]) for i, (src, mid, dst) in enumerate(steps)]
    for cp in loads:
        cp.start()
    for first, then in zip(loads, stores):
        first.wait()
        then.start()
    for cp in stores:
        cp.wait()


def per_device(ne, nz, nk, flows, importer_factor, week_factor):
    ri, rj = flows.shape[1], flows.shape[2]
    nq = ne * nk
    gs = H // nq
    yc = ri // nk
    vm = functools.partial(pltpu.VMEM, dtype=f32)
    shapes = (
        jax.ShapeDtypeStruct((ri, R), f32),
        jax.ShapeDtypeStruct((rj, R), f32),
        jax.ShapeDtypeStruct((1, R), f32),
    )
    outs = pl.pallas_call(
        functools.partial(kernel, ne, nz, nk),
        out_shape=shapes,
        in_specs=[pl.BlockSpec(memory_space=pl.ANY)] * 3,
        out_specs=[pl.BlockSpec(memory_space=pl.ANY)] * 3,
        scratch_shapes=[
            vm((ri, rj)),
            vm((rj, R)),
            vm((1, R)),
            vm((nk, yc, rj)),
            vm((2, yc, H)),
            vm((2 * nz, yc // nz, H)),
            vm((2, yc, H)),
            vm((nq, 1, rj)),
            vm((nk, 1, R)),
            vm((2, H, H)),
            vm((2, 2, gs + STATS, H)),
            vm((2, gs + STATS, H)),
            vm((2, nz, gs + STATS, H)),
            vm((2, 2, nq, gs + STATS, H)),
            vm((nq, gs + 1, H)),
            vm((nq, gs + 1, H)),
            vm((2, H, H)),
            vm((nq, rj // nq, R)),
            vm((nq, rj // nq, R)),
            vm((nq, rj // nq, R)),
            vm((yc, nk * rj)),
            vm((2, nk, yc, H)),
            vm((ri, R)),
            vm((rj, R)),
            vm((1, R)),
            pltpu.SemaphoreType.DMA((NSEM,)),
            pltpu.SemaphoreType.DMA((NSEM,)),
            pltpu.SemaphoreType.DMA((6,)),
        ],
        compiler_params=pltpu.CompilerParams(
            collective_id=0, has_side_effects=True, vmem_limit_bytes=60 * 1024 * 1024
        ),
    )(flows, importer_factor, week_factor)
    return pl.pallas_call(
        hand_over,
        out_shape=shapes,
        in_specs=[pl.BlockSpec(memory_space=pl.ANY)] * 3,
        out_specs=[pl.BlockSpec(memory_space=pl.ANY)] * 3,
        scratch_shapes=[vm((ri, R)), vm((rj, R)), vm((1, R))] + [pltpu.SemaphoreType.DMA((PARTS + 2,))] * 2,
    )(*outs)


def solution(mesh):
    in_specs = (P("wk", "exp", "imp"), P("imp", None), P("wk", None))
    out_specs = (P("exp", None), P("imp", None), P("wk", None))
    fn = functools.partial(per_device, mesh.shape["exp"], mesh.shape["imp"] // 2, mesh.shape["wk"])
    return jax.shard_map(fn, mesh=mesh, in_specs=in_specs, out_specs=out_specs, check_vma=False)
```

```python
import functools

import jax
import jax.numpy as jnp
from jax import lax
from jax.experimental import pallas as pl
from jax.experimental.pallas import tpu as pltpu
from jax.sharding import PartitionSpec as P

ridge = 0.2
eps = 1e-06
hp = lax.Precision.HIGHEST
f32 = jnp.float32
bf16 = jnp.bfloat16
R = 256
H = 128
MESH = pl.DeviceIdType.MESH
STATS = 5
STEPS = 7


def dot(a, b, ca=1, cb=0):
    return lax.dot_general(a, b, (((ca,), (cb,)), ((), ())), precision=hp, preferred_element_type=f32)


def split(a):
    hi = a.astype(bf16)
    return hi, (a - hi.astype(f32)).astype(bf16)


def dot3(a, b):
    ah, al = a
    bh, bl = b
    d = functools.partial(jnp.dot, preferred_element_type=f32)
    return d(ah, bh) + (d(ah, bl) + d(al, bh))


def eye():
    return (lax.broadcasted_iota(jnp.int32, (R, R), 0) == lax.broadcasted_iota(jnp.int32, (R, R), 1)).astype(f32)


def nearly(h):
    one = eye()
    lam = ridge * jnp.sum(h * one) / R
    v = h + lam * one
    top = 1.0 + R / ridge
    alpha = 2.0 / (lam * (1.0 + top))
    delta = (top - 1.0) / (top + 1.0)
    e = one - alpha * v
    for step in range(STEPS):
        c = 2.0 / (2.0 - delta * delta)
        delta = delta * delta / (2.0 - delta * delta)
        se = split(e)
        x = (c * alpha) * (one + e) if step == 0 else c * (x + dot3(split(x), se))
        if step < STEPS - 1:
            e = c * dot3(se, se) + (1.0 - c) * one
    return v, x


def inverse(h):
    v, x = nearly(h)
    return x + dot3(split(x), split(eye() - dot(v, x)))


def solve(m, h):
    v, x = nearly(h)
    x = split(x)
    y = dot3(split(m), x)
    return y + dot3(split(m - dot(y, v)), x)


def triangle():
    r = lax.broadcasted_iota(jnp.int32, (H, H), 0)
    c = lax.broadcasted_iota(jnp.int32, (H, H), 1)
    return r, c


def pack(g):
    r, c = triangle()
    g11 = g[H:, H:]
    return jnp.where(r <= c, g[:H, :H], g11), g[:H, H:], jnp.sum(jnp.where(r == c, g11, 0.0), axis=0, keepdims=True)


def unpack(p0, p1, d):
    r, c = triangle()
    g00 = jnp.where(r <= c, p0, 0.0) + jnp.where(r < c, p0, 0.0).T
    low = jnp.where(r > c, p0, 0.0)
    g11 = low + low.T + jnp.where(r == c, d, 0.0)
    return jnp.concatenate(
        [jnp.concatenate([g00, p1], axis=1), jnp.concatenate([p1.T, g11], axis=1)], axis=0)


def kernel(ne, nz, nk, f_hbm, b_hbm, w_hbm, a_hbm, b_out_hbm, c_hbm,
           f_ref, b_ref, w_ref, fa, u, c_in, z_in, ma, cq, wx,
           pk, cs, ci, zi, xs, gi, gx, gag, mi, mo, mos, res, raw, a_out, b_out, c_out,
           ssem, rsem, lsem):
    e = lax.axis_index("exp")
    p = lax.axis_index("imp")
    k = lax.axis_index("wk")
    z = lax.div(p, 2)
    c = lax.rem(p, 2)
    o = 1 - c
    nq = ne * nk
    q = e * nk + k
    ri, rj = f_ref.shape
    yc = ri // nk
    zc = yc // nz
    jc = rj // nq
    gs = H // nq
    used = [0]
    pending = []

    loads = [pltpu.make_async_copy(f_hbm.at[0], f_ref, lsem.at[0]),
             pltpu.make_async_copy(b_hbm, b_ref, lsem.at[1]),
             pltpu.make_async_copy(w_hbm, w_ref, lsem.at[2])]
    for cp in loads:
        cp.start()
    stores = [pltpu.make_async_copy(src, dst, lsem.at[3 + i])
              for i, (src, dst) in enumerate([(a_out, a_hbm), (b_out, b_out_hbm), (c_out, c_hbm)])]

    def take():
        used[0] += 1
        return used[0] - 1

    def remote(src, dst, s, dev):
        return pltpu.make_async_remote_copy(
            src_ref=src, dst_ref=dst, send_sem=ssem.at[s], recv_sem=rsem.at[s],
            device_id=dev, device_id_type=MESH)

    core_dev = {"imp": z * 2 + o}

    def push_core(src, dst):
        cp = remote(src, dst, take(), core_dev)
        cp.start()
        pending.append(cp.wait_send)
        return cp.wait_recv

    def push_group(n, dev, src, dst, every, first=1):
        s = take()

        def go(i, carry):
            d = far(i, n)
            remote(src(d), dst, s, dev(d)).start()
            return carry

        lax.fori_loop(0, n - first, go, 0)
        cp = remote(every, every, s, dev(1))
        pending.append(cp.wait_send)
        return cp.wait_recv

    def push_both(n, dev, dev_o, src, src_o, dst, every, every_o):
        s, s_o = take(), take()

        def go(i, carry):
            d = far(i, n)
            remote(src(d), dst, s, dev(d)).start()
            remote(src_o(d), dst, s_o, dev_o(d)).start()
            return carry

        lax.fori_loop(0, n - 1, go, 0)
        remote(src_o(0), dst, s_o, dev_o(0)).start()
        cp = remote(every, every, s, dev(1))
        cp_o = remote(every_o, every_o, s_o, dev_o(0))
        pending.extend([cp.wait_send, cp_o.wait_send])

        def wait():
            cp.wait_recv()
            cp_o.wait_recv()

        return wait

    def far(i, n):
        h = lax.div(i + 1, 2)
        return lax.rem(n // 2 + jnp.where(lax.rem(i, 2) == 1, h, -h), n)

    def zto(d):
        return lax.rem(z + d, nz)

    def zdev(d):
        return {"imp": zto(d) * 2 + c}

    def zodev(d):
        return {"imp": zto(d) * 2 + o}

    def yto(d):
        return lax.rem(k + d, nk)

    def ydev(d):
        return {"wk": yto(d)}

    def qto(d):
        return lax.rem(q + d, nq)

    def qdev(d):
        return {"exp": lax.div(qto(d), nk), "wk": lax.rem(qto(d), nk)}

    def odev(d):
        return {"exp": lax.div(qto(d), nk), "wk": lax.rem(qto(d), nk), "imp": z * 2 + o}

    barrier = pltpu.get_barrier_semaphore()
    def greet(n, first, dev):
        def one_device(i, carry):
            pl.semaphore_signal(barrier, inc=1, device_id=dev(far(i, n)), device_id_type=MESH)
            return carry

        lax.fori_loop(0, n - first, one_device, 0)

    greet(nz, 1, zdev)
    greet(nq, 1, qdev)
    greet(nq, 0, odev)

    def chain_fill(n, gram, stats):
        p0, p1, d = pack(gram)
        pk[0, :, :] = p0
        pk[1, :, :] = p1
        for h in range(2):
            cs[n, h, 0:gs, :] = pk[h, pl.ds(pl.multiple_of(q * gs, gs), gs), :]
            cs[n, h, gs:gs + 1, :] = d
            for s, row in enumerate(stats):
                cs[n, h, gs + 1 + s:gs + 2 + s, :] = row[:, h * H:(h + 1) * H]
            for s in range(len(stats), STATS - 1):
                cs[n, h, gs + 1 + s:gs + 2 + s, :] = jnp.zeros((1, H), f32)

    def chain_core(n):
        return push_core(cs.at[n, o], ci.at[n])

    def chain_z(n):
        zi[n, z, :, :] = cs[n, c] + ci[n]
        return push_group(nz, zdev, lambda d: zi.at[n, z], zi.at[n, z], zi.at[n, pl.ds(0, nz - 1)])

    def chain_q(n):
        xs[n, c, q, :, :] = jnp.sum(zi[n], axis=0)
        mine = xs.at[n, c, q]
        return push_both(nq, qdev, odev, lambda d: mine, lambda d: mine, mine, xs.at[n, c, pl.ds(0, nq - 1)], xs.at[n, c])

    def chain_gram(n):
        return unpack(xs[n, 0, :, 0:gs, :].reshape(H, H), xs[n, 1, :, 0:gs, :].reshape(H, H), xs[n, 0, 0, gs:gs + 1, :])

    def chain_stat(n, qq, s):
        return jnp.concatenate([xs[n, h, qq, gs + 1 + s:gs + 2 + s, :] for h in range(2)], axis=1)

    def add(terms):
        tot = terms[0]
        for term in terms[1:]:
            tot = tot + term
        return tot

    for cp in loads:
        cp.wait()
    f = f_ref[...]
    b = b_ref[...]
    w = w_ref[...]
    shifted = b - 0.5
    wx[k, :, :] = w
    rowp = dot(jnp.ones((8, rj), f32), f, 1, 1)
    colp = jnp.sum(f, axis=0, keepdims=True)
    cq[q, :, :] = colp
    v = dot(jnp.broadcast_to(colp, (8, rj)), shifted)[0:1]
    chain_fill(0, dot(b, b, 0, 0), [v] + [rowp[0:1, i * R:(i + 1) * R] for i in range(ri // R)])
    fa[k, :, :] = f_ref[pl.ds(pl.multiple_of(k * yc, yc), yc), :]

    pl.semaphore_wait(barrier, (nz - 1) + (nq - 1) + nq)

    w_f = push_group(nk, ydev, lambda d: f_ref.at[pl.ds(pl.multiple_of(yto(d) * yc, yc), yc)], fa.at[k], fa.at[pl.ds(0, nk - 1)])
    w_cs = chain_core(0)
    w_w = push_group(nk, ydev, lambda d: wx.at[k], wx.at[k], wx.at[pl.ds(0, nk - 1)])
    w_cs()
    w_z = chain_z(0)
    w_c = push_group(nq, qdev, lambda d: cq.at[q], cq.at[q], cq.at[pl.ds(0, nq - 1)])

    w_w()
    ws = jnp.concatenate([wx[i] for i in range(nk)] + [jnp.zeros((8 - nk, R), f32)], axis=0)
    gram_c = dot(ws, ws, 0, 0)
    w_f()
    g = dot(fa[...].reshape(ri, rj), shifted)
    gw = add([g[i * yc:(i + 1) * yc] * ws[i:i + 1] for i in range(nk)])
    u[0, :, :] = gw[:, 0:H]
    u[1, :, :] = gw[:, H:R]
    def cut(h, zz):
        return u.at[h, pl.ds(pl.multiple_of(zz * zc, zc), zc)]

    w_u = push_core(u.at[o], c_in)
    w_u()
    u[c, :, :] = u[c] + c_in[...]
    z_in[z, :, :] = cut(c, z)[...]
    w_z3 = push_group(nz, zdev, lambda d: cut(c, zto(d)), z_in.at[z], z_in.at[pl.ds(0, nz - 1)])
    w_z()
    w_q = chain_q(0)
    w_z3()
    tile = ma.at[c, pl.ds(pl.multiple_of(z * zc, zc), zc)]
    tile[...] = jnp.sum(z_in[...], axis=0)
    w_z4 = push_group(nz, zdev, lambda d: tile, tile, ma.at[c, pl.ds(0, yc - zc)])
    w_q()
    h1 = chain_gram(0) * gram_c
    one = eye()
    x1 = inverse(h1)

    w_c()
    zero = jnp.zeros((1, R), f32)
    pad = [jnp.zeros((1, H), f32)] * (8 - nk)
    seg, half = lax.div(k, 2), lax.rem(k, 2)
    coef, totals, cols = [], [], []
    for kk in range(nk):
        grand = add([jnp.sum(chain_stat(0, ee * nk + kk, 1 + i), axis=1, keepdims=True)
                     for ee in range(ne) for i in range(ri // R)])
        coef.append(add([chain_stat(0, ee * nk + kk, 0) for ee in range(ne)]) * ws[kk:kk + 1] / grand)
        totals.append(xs[0, half, e * nk + kk, pl.ds(gs + 2 + seg, 1), :])
        cols.append(add([cq[ee * nk + kk] for ee in range(ne)]) / grand)
    coef = jnp.concatenate(coef + [zero] * (8 - nk), axis=0)
    totals = jnp.concatenate(totals + pad, axis=0)
    week = lax.broadcasted_iota(jnp.int32, (8, 1), 0)
    fix = dot(totals, coef, 0, 0)

    w_z4()
    w_m = push_core(ma.at[c], ma.at[c])
    w_m()
    raw_a = dot(jnp.concatenate([ma[0], ma[1]], axis=1) - fix, x1)

    p0, p1, d = pack(dot(raw_a, raw_a, 0, 0))
    pk[0, :, :] = p0
    pk[1, :, :] = p1
    for i in range(nq):
        gx[i, 0:gs, :] = pk[c, i * gs:(i + 1) * gs, :]
        gx[i, gs:gs + 1, :] = d
    gi[q, :, :] = gx[q]
    w_gi = push_group(nq, qdev, lambda d: gx.at[qto(d)], gi.at[q], gi.at[pl.ds(0, nq - 1)])

    for kk in range(nk):
        only = (week == kk).astype(f32)
        res[:, kk * rj:(kk + 1) * rj] = fa[kk] - dot(totals * only, cols[kk] * only, 0, 0)
    t = dot(res[...], raw_a, 0, 0)
    tw = add([t[i * rj:(i + 1) * rj] * ws[i:i + 1] for i in range(nk)])
    for i in range(nq):
        mos[i, :, :] = tw[i * jc:(i + 1) * jc]
    mi[q, :, :] = mos[q]
    w_mi = push_group(nq, qdev, lambda d: mos.at[qto(d)], mi.at[q], mi.at[pl.ds(0, nq - 1)])
    raw[0, k, :, :] = raw_a[:, 0:H]
    raw[1, k, :, :] = raw_a[:, H:R]

    w_gi()
    gsum = jnp.sum(gi[...], axis=0)
    mine = gag.at[c, pl.ds(pl.multiple_of(q * gs, gs), gs)]
    mine[...] = gsum[0:gs]
    w_ga = push_both(nq, qdev, odev, lambda d: mine, lambda d: mine, mine, gag.at[c, pl.ds(0, H - gs)], gag.at[c])
    w_mi()
    mo[q, :, :] = jnp.sum(mi[...], axis=0)
    w_mo = push_group(nq, qdev, lambda d: mo.at[q], mo.at[q], mo.at[pl.ds(0, nq - 1)])
    w_ga()
    w_raw = push_group(nk, ydev, lambda d: raw.at[c, k], raw.at[c, k], raw.at[c, pl.ds(0, nk - 1)])
    gram_a = unpack(gag[0], gag[1], gsum[gs:gs + 1])

    def unscale(gram, count):
        d = gram * one
        inv_row = 1.0 / jnp.sqrt(jnp.sum(d, axis=0, keepdims=True) / count + eps)
        inv_col = 1.0 / jnp.sqrt(jnp.sum(d, axis=1, keepdims=True) / count + eps)
        return inv_row, gram * inv_row * inv_col

    sa, gram_a = unscale(gram_a, ri * ne)
    h2 = gram_a * gram_c
    w_mo()
    raw_b = solve(mo[...].reshape(rj, R) * sa, h2)

    chain_fill(1, dot(raw_b, raw_b, 0, 0),
               [jnp.sum(t[i * rj:(i + 1) * rj] * raw_b, axis=0, keepdims=True) for i in range(nk)])
    w_cs = chain_core(1)
    w_cs()
    w_z = chain_z(1)
    w_raw()
    w_rc = push_core(raw.at[c], raw.at[c])
    w_rc()
    a_out[:, 0:H] = raw[0].reshape(ri, H) * sa[:, 0:H]
    a_out[:, H:R] = raw[1].reshape(ri, H) * sa[:, H:R]
    stores[0].start()
    w_z()
    w_q = chain_q(1)
    w_q()
    sb, gram_b2 = unscale(chain_gram(1), rj * nz * 2)
    b_out[...] = raw_b * sb
    stores[1].start()
    h3 = gram_a * gram_b2
    scale = sa * sb
    m_c = jnp.concatenate([add([chain_stat(1, qq, kk) for qq in range(nq)]) * scale for kk in range(nk)] + [zero] * (8 - nk), axis=0)
    raw_c = solve(m_c, h3)
    sc = jnp.sqrt(jnp.sum(raw_c * raw_c, axis=0, keepdims=True) / nk + eps)
    c_out[...] = jnp.sum(raw_c * (week == k).astype(f32), axis=0, keepdims=True) / sc
    stores[2].start()

    for fin in pending:
        fin()
    for cp in stores:
        cp.wait()
    assert used[0] == NSEM


NSEM = 22
PARTS = 4


def hand_over(a_in, b_in, c_in, a_out, b_out, c_out, a, b, c, load, store):
    rows = a_in.shape[0] // PARTS
    steps = [(x_in.at[pl.ds(i * n, n)], x.at[pl.ds(i * n, n)], x_out.at[pl.ds(i * n, n)])
             for x_in, x, x_out, n, parts in ((a_in, a, a_out, rows, PARTS), (b_in, b, b_out, b_in.shape[0], 1))
             for i in range(parts)] + [(c_in, c, c_out)]
    loads = [pltpu.make_async_copy(src, mid, load.at[i]) for i, (src, mid, dst) in enumerate(steps)]
    stores = [pltpu.make_async_copy(mid, dst, store.at[i]) for i, (src, mid, dst) in enumerate(steps)]
    for cp in loads:
        cp.start()
    for first, then in zip(loads, stores):
        first.wait()
        then.start()
    for cp in stores:
        cp.wait()


def per_device(ne, nz, nk, flows, importer_factor, week_factor):
    ri, rj = flows.shape[1], flows.shape[2]
    nq = ne * nk
    gs = H // nq
    yc = ri // nk
    vm = functools.partial(pltpu.VMEM, dtype=f32)
    shapes = (
        jax.ShapeDtypeStruct((ri, R), f32),
        jax.ShapeDtypeStruct((rj, R), f32),
        jax.ShapeDtypeStruct((1, R), f32),
    )
    outs = pl.pallas_call(
        functools.partial(kernel, ne, nz, nk),
        out_shape=shapes,
        in_specs=[pl.BlockSpec(memory_space=pl.ANY)] * 3,
        out_specs=[pl.BlockSpec(memory_space=pl.ANY)] * 3,
        scratch_shapes=[
            vm((ri, rj)),
            vm((rj, R)),
            vm((1, R)),
            vm((nk, yc, rj)),
            vm((2, yc, H)),
            vm((yc, H)),
            vm((nz, yc // nz, H)),
            vm((2, yc, H)),
            vm((nq, 1, rj)),
            vm((nk, 1, R)),
            vm((2, H, H)),
            vm((2, 2, gs + STATS, H)),
            vm((2, gs + STATS, H)),
            vm((2, nz, gs + STATS, H)),
            vm((2, 2, nq, gs + STATS, H)),
            vm((nq, gs + 1, H)),
            vm((nq, gs + 1, H)),
            vm((2, H, H)),
            vm((nq, rj // nq, R)),
            vm((nq, rj // nq, R)),
            vm((nq, rj // nq, R)),
            vm((yc, nk * rj)),
            vm((2, nk, yc, H)),
            vm((ri, R)),
            vm((rj, R)),
            vm((1, R)),
            pltpu.SemaphoreType.DMA((NSEM,)),
            pltpu.SemaphoreType.DMA((NSEM,)),
            pltpu.SemaphoreType.DMA((6,)),
        ],
        compiler_params=pltpu.CompilerParams(
            collective_id=0, has_side_effects=True, vmem_limit_bytes=60 * 1024 * 1024
        ),
    )(flows, importer_factor, week_factor)
    return pl.pallas_call(
        hand_over,
        out_shape=shapes,
        in_specs=[pl.BlockSpec(memory_space=pl.ANY)] * 3,
        out_specs=[pl.BlockSpec(memory_space=pl.ANY)] * 3,
        scratch_shapes=[vm((ri, R)), vm((rj, R)), vm((1, R))] + [pltpu.SemaphoreType.DMA((PARTS + 2,))] * 2,
    )(*outs)


def solution(mesh):
    in_specs = (P("wk", "exp", "imp"), P("imp", None), P("wk", None))
    out_specs = (P("exp", None), P("imp", None), P("wk", None))
    fn = functools.partial(per_device, mesh.shape["exp"], mesh.shape["imp"] // 2, mesh.shape["wk"])
    return jax.shard_map(fn, mesh=mesh, in_specs=in_specs, out_specs=out_specs, check_vma=False)
```

```python
import functools

import jax
import jax.numpy as jnp
from jax import lax
from jax.experimental import pallas as pl
from jax.experimental.pallas import tpu as pltpu
from jax.sharding import PartitionSpec as P

ridge = 0.2
eps = 1e-06
hp = lax.Precision.HIGHEST
f32 = jnp.float32
bf16 = jnp.bfloat16
R = 256
H = 128
MESH = pl.DeviceIdType.MESH
STATS = 5
STEPS = 7


def dot(a, b, ca=1, cb=0):
    return lax.dot_general(a, b, (((ca,), (cb,)), ((), ())), precision=hp, preferred_element_type=f32)


def split(a):
    hi = a.astype(bf16)
    return hi, (a - hi.astype(f32)).astype(bf16)


def dot3(a, b):
    ah, al = a
    bh, bl = b
    d = functools.partial(jnp.dot, preferred_element_type=f32)
    return d(ah, bh) + (d(ah, bl) + d(al, bh))


def eye():
    return (lax.broadcasted_iota(jnp.int32, (R, R), 0) == lax.broadcasted_iota(jnp.int32, (R, R), 1)).astype(f32)


def nearly(h):
    one = eye()
    lam = ridge * jnp.sum(h * one) / R
    v = h + lam * one
    top = 1.0 + R / ridge
    alpha = 2.0 / (lam * (1.0 + top))
    delta = (top - 1.0) / (top + 1.0)
    e = one - alpha * v
    for step in range(STEPS):
        c = 2.0 / (2.0 - delta * delta)
        delta = delta * delta / (2.0 - delta * delta)
        se = split(e)
        x = (c * alpha) * (one + e) if step == 0 else c * (x + dot3(split(x), se))
        if step < STEPS - 1:
            e = c * dot3(se, se) + (1.0 - c) * one
    return v, x


def inverse(h):
    v, x = nearly(h)
    return x + dot3(split(x), split(eye() - dot(v, x)))


def solve(m, h):
    v, x = nearly(h)
    x = split(x)
    y = dot3(split(m), x)
    return y + dot3(split(m - dot(y, v)), x)


def triangle():
    r = lax.broadcasted_iota(jnp.int32, (H, H), 0)
    c = lax.broadcasted_iota(jnp.int32, (H, H), 1)
    return r, c


def pack(g):
    r, c = triangle()
    g11 = g[H:, H:]
    return jnp.where(r <= c, g[:H, :H], g11), g[:H, H:], jnp.sum(jnp.where(r == c, g11, 0.0), axis=0, keepdims=True)


def unpack(p0, p1, d):
    r, c = triangle()
    g00 = jnp.where(r <= c, p0, 0.0) + jnp.where(r < c, p0, 0.0).T
    low = jnp.where(r > c, p0, 0.0)
    g11 = low + low.T + jnp.where(r == c, d, 0.0)
    return jnp.concatenate(
        [jnp.concatenate([g00, p1], axis=1), jnp.concatenate([p1.T, g11], axis=1)], axis=0)


def kernel(ne, nz, nk, f_hbm, b_hbm, w_hbm, a_hbm, b_out_hbm, c_hbm,
           f_ref, b_ref, w_ref, fa, u, c_in, zb, vs, z_in, ma, cq, wx,
           pk, cs, ci, zi, xs, gi, gx, gag, mi, mo, mos, res, raw, a_out, b_out, c_out,
           ssem, rsem, lsem):
    e = lax.axis_index("exp")
    p = lax.axis_index("imp")
    k = lax.axis_index("wk")
    z = lax.div(p, 2)
    c = lax.rem(p, 2)
    o = 1 - c
    nq = ne * nk
    q = e * nk + k
    ri, rj = f_ref.shape
    yc = ri // nk
    zc = yc // nz
    jc = rj // nq
    gs = H // nq
    used = [0]
    pending = []

    loads = [pltpu.make_async_copy(f_hbm.at[0], f_ref, lsem.at[0]),
             pltpu.make_async_copy(b_hbm, b_ref, lsem.at[1]),
             pltpu.make_async_copy(w_hbm, w_ref, lsem.at[2])]
    for cp in loads:
        cp.start()
    stores = [pltpu.make_async_copy(src, dst, lsem.at[3 + i])
              for i, (src, dst) in enumerate([(a_out, a_hbm), (b_out, b_out_hbm), (c_out, c_hbm)])]

    def take():
        used[0] += 1
        return used[0] - 1

    def remote(src, dst, s, dev):
        return pltpu.make_async_remote_copy(
            src_ref=src, dst_ref=dst, send_sem=ssem.at[s], recv_sem=rsem.at[s],
            device_id=dev, device_id_type=MESH)

    core_dev = {"imp": z * 2 + o}

    def push_core(src, dst):
        cp = remote(src, dst, take(), core_dev)
        cp.start()
        pending.append(cp.wait_send)
        return cp.wait_recv

    def push_group(n, dev, src, dst, every, first=1):
        s = take()

        def go(i, carry):
            d = far(i, n)
            remote(src(d), dst, s, dev(d)).start()
            return carry

        lax.fori_loop(0, n - first, go, 0)
        cp = remote(every, every, s, dev(1))
        pending.append(cp.wait_send)
        return cp.wait_recv

    def push_both(n, dev, dev_o, src, src_o, dst, every, every_o):
        s, s_o = take(), take()

        def go(i, carry):
            d = far(i, n)
            remote(src(d), dst, s, dev(d)).start()
            remote(src_o(d), dst, s_o, dev_o(d)).start()
            return carry

        lax.fori_loop(0, n - 1, go, 0)
        remote(src_o(0), dst, s_o, dev_o(0)).start()
        cp = remote(every, every, s, dev(1))
        cp_o = remote(every_o, every_o, s_o, dev_o(0))
        pending.extend([cp.wait_send, cp_o.wait_send])

        def wait():
            cp.wait_recv()
            cp_o.wait_recv()

        return wait

    def far(i, n):
        h = lax.div(i + 1, 2)
        return lax.rem(n // 2 + jnp.where(lax.rem(i, 2) == 1, h, -h), n)

    def zto(d):
        return lax.rem(z + d, nz)

    def zdev(d):
        return {"imp": zto(d) * 2 + c}

    def zodev(d):
        return {"imp": zto(d) * 2 + o}

    def yto(d):
        return lax.rem(k + d, nk)

    def ydev(d):
        return {"wk": yto(d)}

    def qto(d):
        return lax.rem(q + d, nq)

    def qdev(d):
        return {"exp": lax.div(qto(d), nk), "wk": lax.rem(qto(d), nk)}

    def odev(d):
        return {"exp": lax.div(qto(d), nk), "wk": lax.rem(qto(d), nk), "imp": z * 2 + o}

    barrier = pltpu.get_barrier_semaphore()
    def greet(n, first, dev):
        def one_device(i, carry):
            pl.semaphore_signal(barrier, inc=1, device_id=dev(far(i, n)), device_id_type=MESH)
            return carry

        lax.fori_loop(0, n - first, one_device, 0)

    greet(nz, 1, zdev)
    greet(nz, 0, zodev)
    greet(nq, 1, qdev)
    greet(nq, 1, odev)

    def chain_fill(n, gram, stats):
        p0, p1, d = pack(gram)
        pk[0, :, :] = p0
        pk[1, :, :] = p1
        for h in range(2):
            cs[n, h, 0:gs, :] = pk[h, pl.ds(pl.multiple_of(q * gs, gs), gs), :]
            cs[n, h, gs:gs + 1, :] = d
            for s, row in enumerate(stats):
                cs[n, h, gs + 1 + s:gs + 2 + s, :] = row[:, h * H:(h + 1) * H]
            for s in range(len(stats), STATS - 1):
                cs[n, h, gs + 1 + s:gs + 2 + s, :] = jnp.zeros((1, H), f32)

    def chain_core(n):
        return push_core(cs.at[n, o], ci.at[n])

    def chain_z(n):
        zi[n, z, :, :] = cs[n, c] + ci[n]
        return push_group(nz, zdev, lambda d: zi.at[n, z], zi.at[n, z], zi.at[n, pl.ds(0, nz - 1)])

    def chain_q(n):
        xs[n, c, q, :, :] = jnp.sum(zi[n], axis=0)
        if n == 0:
            xs[n, c, q, gs + 1:gs + 2, :] = xs[n, c, q, gs + 1:gs + 2, :] + vs[c]
        mine = xs.at[n, c, q]
        return push_both(nq, qdev, odev, lambda d: mine, lambda d: mine, mine, xs.at[n, c, pl.ds(0, nq - 1)], xs.at[n, c])

    def chain_gram(n):
        return unpack(xs[n, 0, :, 0:gs, :].reshape(H, H), xs[n, 1, :, 0:gs, :].reshape(H, H), xs[n, 0, 0, gs:gs + 1, :])

    def chain_stat(n, qq, s):
        return jnp.concatenate([xs[n, h, qq, gs + 1 + s:gs + 2 + s, :] for h in range(2)], axis=1)

    def add(terms):
        tot = terms[0]
        for term in terms[1:]:
            tot = tot + term
        return tot

    for cp in loads:
        cp.wait()
    f = f_ref[...]
    b = b_ref[...]
    w = w_ref[...]
    own = jnp.sum(b, axis=0, keepdims=True) / rj
    shifted = b - own
    wx[k, :, :] = w
    rowp = dot(jnp.ones((8, rj), f32), f, 1, 1)
    colp = jnp.sum(f, axis=0, keepdims=True)
    cq[q, :, :] = colp
    zb[p, 0:1, :] = own
    zb[p, 1:2, :] = jnp.broadcast_to(jnp.sum(colp, axis=1, keepdims=True), (1, R))
    v = dot(jnp.broadcast_to(colp, (8, rj)), shifted)[0:1]
    chain_fill(0, dot(b, b, 0, 0), [v] + [rowp[0:1, i * R:(i + 1) * R] for i in range(ri // R)])
    fa[k, :, :] = f_ref[pl.ds(pl.multiple_of(k * yc, yc), yc), :]

    pl.semaphore_wait(barrier, (nz - 1) + nz + 2 * (nq - 1))

    w_f = push_group(nk, ydev, lambda d: f_ref.at[pl.ds(pl.multiple_of(yto(d) * yc, yc), yc)], fa.at[k], fa.at[pl.ds(0, nk - 1)])
    w_cs = chain_core(0)
    w_zb = push_both(nz, zdev, zodev, lambda d: zb.at[p], lambda d: zb.at[p], zb.at[p],
                     zb.at[pl.ds(0, nz - 1)], zb.at[pl.ds(0, nz)])
    w_w = push_group(nk, ydev, lambda d: wx.at[k], wx.at[k], wx.at[pl.ds(0, nk - 1)])
    w_cs()
    w_z = chain_z(0)
    w_c = push_group(nq, qdev, lambda d: cq.at[q], cq.at[q], cq.at[pl.ds(0, nq - 1)])

    w_w()
    ws = jnp.concatenate([wx[i] for i in range(nk)] + [jnp.zeros((8 - nk, R), f32)], axis=0)
    gram_c = dot(ws, ws, 0, 0)
    w_f()
    g = dot(fa[...].reshape(ri, rj), shifted)
    here = [jnp.sum(fa[i], axis=1, keepdims=True) for i in range(nk)]
    w_zb()
    means = zb[:, 0, :]
    mean = jnp.sum(means, axis=0, keepdims=True) / (2 * nz)
    off = own - mean
    moved = jnp.sum((means - mean) * zb[:, 1, :], axis=0, keepdims=True)
    vs[0, :, :] = moved[:, 0:H]
    vs[1, :, :] = moved[:, H:R]
    gw = add([(g[i * yc:(i + 1) * yc] + here[i] * off) * ws[i:i + 1] for i in range(nk)])
    u[0, :, :] = gw[:, 0:H]
    u[1, :, :] = gw[:, H:R]
    def cut(h, zz):
        return u.at[h, pl.ds(pl.multiple_of(zz * zc, zc), zc)]

    w_u = push_core(u.at[o], c_in)
    w_u()
    u[c, :, :] = u[c] + c_in[...]
    z_in[z, :, :] = cut(c, z)[...]
    w_z3 = push_group(nz, zdev, lambda d: cut(c, zto(d)), z_in.at[z], z_in.at[pl.ds(0, nz - 1)])
    w_z()
    w_q = chain_q(0)
    w_z3()
    tile = ma.at[c, pl.ds(pl.multiple_of(z * zc, zc), zc)]
    tile[...] = jnp.sum(z_in[...], axis=0)
    w_z4 = push_group(nz, zdev, lambda d: tile, tile, ma.at[c, pl.ds(0, yc - zc)])
    w_q()
    h1 = chain_gram(0) * gram_c
    one = eye()
    x1 = inverse(h1)

    w_c()
    zero = jnp.zeros((1, R), f32)
    pad = [jnp.zeros((1, H), f32)] * (8 - nk)
    seg, half = lax.div(k, 2), lax.rem(k, 2)
    coef, totals, cols = [], [], []
    for kk in range(nk):
        grand = add([jnp.sum(chain_stat(0, ee * nk + kk, 1 + i), axis=1, keepdims=True)
                     for ee in range(ne) for i in range(ri // R)])
        coef.append(add([chain_stat(0, ee * nk + kk, 0) for ee in range(ne)]) * ws[kk:kk + 1] / grand)
        totals.append(xs[0, half, e * nk + kk, pl.ds(gs + 2 + seg, 1), :])
        cols.append(add([cq[ee * nk + kk] for ee in range(ne)]) / grand)
    coef = jnp.concatenate(coef + [zero] * (8 - nk), axis=0)
    totals = jnp.concatenate(totals + pad, axis=0)
    week = lax.broadcasted_iota(jnp.int32, (8, 1), 0)
    fix = dot(totals, coef, 0, 0)

    w_z4()
    w_m = push_core(ma.at[c], ma.at[c])
    w_m()
    raw_a = dot(jnp.concatenate([ma[0], ma[1]], axis=1) - fix, x1)

    p0, p1, d = pack(dot(raw_a, raw_a, 0, 0))
    pk[0, :, :] = p0
    pk[1, :, :] = p1
    for i in range(nq):
        gx[i, 0:gs, :] = pk[c, i * gs:(i + 1) * gs, :]
        gx[i, gs:gs + 1, :] = d
    gi[q, :, :] = gx[q]
    w_gi = push_group(nq, qdev, lambda d: gx.at[qto(d)], gi.at[q], gi.at[pl.ds(0, nq - 1)])

    for kk in range(nk):
        only = (week == kk).astype(f32)
        res[:, kk * rj:(kk + 1) * rj] = fa[kk] - dot(totals * only, cols[kk] * only, 0, 0)
    t = dot(res[...], raw_a, 0, 0)
    tw = add([t[i * rj:(i + 1) * rj] * ws[i:i + 1] for i in range(nk)])
    for i in range(nq):
        mos[i, :, :] = tw[i * jc:(i + 1) * jc]
    mi[q, :, :] = mos[q]
    w_mi = push_group(nq, qdev, lambda d: mos.at[qto(d)], mi.at[q], mi.at[pl.ds(0, nq - 1)])
    raw[0, k, :, :] = raw_a[:, 0:H]
    raw[1, k, :, :] = raw_a[:, H:R]

    w_gi()
    gsum = jnp.sum(gi[...], axis=0)
    mine = gag.at[c, pl.ds(pl.multiple_of(q * gs, gs), gs)]
    mine[...] = gsum[0:gs]
    w_ga = push_both(nq, qdev, odev, lambda d: mine, lambda d: mine, mine, gag.at[c, pl.ds(0, H - gs)], gag.at[c])
    w_mi()
    mo[q, :, :] = jnp.sum(mi[...], axis=0)
    w_mo = push_group(nq, qdev, lambda d: mo.at[q], mo.at[q], mo.at[pl.ds(0, nq - 1)])
    w_ga()
    w_raw = push_group(nk, ydev, lambda d: raw.at[c, k], raw.at[c, k], raw.at[c, pl.ds(0, nk - 1)])
    gram_a = unpack(gag[0], gag[1], gsum[gs:gs + 1])

    def unscale(gram, count):
        d = gram * one
        inv_row = 1.0 / jnp.sqrt(jnp.sum(d, axis=0, keepdims=True) / count + eps)
        inv_col = 1.0 / jnp.sqrt(jnp.sum(d, axis=1, keepdims=True) / count + eps)
        return inv_row, gram * inv_row * inv_col

    sa, gram_a = unscale(gram_a, ri * ne)
    h2 = gram_a * gram_c
    w_mo()
    raw_b = solve(mo[...].reshape(rj, R) * sa, h2)

    chain_fill(1, dot(raw_b, raw_b, 0, 0),
               [jnp.sum(t[i * rj:(i + 1) * rj] * raw_b, axis=0, keepdims=True) for i in range(nk)])
    w_cs = chain_core(1)
    w_cs()
    w_z = chain_z(1)
    w_raw()
    w_rc = push_core(raw.at[c], raw.at[c])
    w_rc()
    a_out[:, 0:H] = raw[0].reshape(ri, H) * sa[:, 0:H]
    a_out[:, H:R] = raw[1].reshape(ri, H) * sa[:, H:R]
    stores[0].start()
    w_z()
    w_q = chain_q(1)
    w_q()
    sb, gram_b2 = unscale(chain_gram(1), rj * nz * 2)
    b_out[...] = raw_b * sb
    stores[1].start()
    h3 = gram_a * gram_b2
    scale = sa * sb
    m_c = jnp.concatenate([add([chain_stat(1, qq, kk) for qq in range(nq)]) * scale for kk in range(nk)] + [zero] * (8 - nk), axis=0)
    raw_c = solve(m_c, h3)
    sc = jnp.sqrt(jnp.sum(raw_c * raw_c, axis=0, keepdims=True) / nk + eps)
    c_out[...] = jnp.sum(raw_c * (week == k).astype(f32), axis=0, keepdims=True) / sc
    stores[2].start()

    for fin in pending:
        fin()
    for cp in stores:
        cp.wait()
    assert used[0] == NSEM


NSEM = 24
PARTS = 4


def hand_over(a_in, b_in, c_in, a_out, b_out, c_out, a, b, c, load, store):
    rows = a_in.shape[0] // PARTS
    steps = [(x_in.at[pl.ds(i * n, n)], x.at[pl.ds(i * n, n)], x_out.at[pl.ds(i * n, n)])
             for x_in, x, x_out, n, parts in ((a_in, a, a_out, rows, PARTS), (b_in, b, b_out, b_in.shape[0], 1))
             for i in range(parts)] + [(c_in, c, c_out)]
    loads = [pltpu.make_async_copy(src, mid, load.at[i]) for i, (src, mid, dst) in enumerate(steps)]
    stores = [pltpu.make_async_copy(mid, dst, store.at[i]) for i, (src, mid, dst) in enumerate(steps)]
    for cp in loads:
        cp.start()
    for first, then in zip(loads, stores):
        first.wait()
        then.start()
    for cp in stores:
        cp.wait()


def per_device(ne, nz, nk, flows, importer_factor, week_factor):
    ri, rj = flows.shape[1], flows.shape[2]
    nq = ne * nk
    gs = H // nq
    yc = ri // nk
    vm = functools.partial(pltpu.VMEM, dtype=f32)
    shapes = (
        jax.ShapeDtypeStruct((ri, R), f32),
        jax.ShapeDtypeStruct((rj, R), f32),
        jax.ShapeDtypeStruct((1, R), f32),
    )
    outs = pl.pallas_call(
        functools.partial(kernel, ne, nz, nk),
        out_shape=shapes,
        in_specs=[pl.BlockSpec(memory_space=pl.ANY)] * 3,
        out_specs=[pl.BlockSpec(memory_space=pl.ANY)] * 3,
        scratch_shapes=[
            vm((ri, rj)),
            vm((rj, R)),
            vm((1, R)),
            vm((nk, yc, rj)),
            vm((2, yc, H)),
            vm((yc, H)),
            vm((2 * nz, 2, R)),
            vm((2, 1, H)),
            vm((nz, yc // nz, H)),
            vm((2, yc, H)),
            vm((nq, 1, rj)),
            vm((nk, 1, R)),
            vm((2, H, H)),
            vm((2, 2, gs + STATS, H)),
            vm((2, gs + STATS, H)),
            vm((2, nz, gs + STATS, H)),
            vm((2, 2, nq, gs + STATS, H)),
            vm((nq, gs + 1, H)),
            vm((nq, gs + 1, H)),
            vm((2, H, H)),
            vm((nq, rj // nq, R)),
            vm((nq, rj // nq, R)),
            vm((nq, rj // nq, R)),
            vm((yc, nk * rj)),
            vm((2, nk, yc, H)),
            vm((ri, R)),
            vm((rj, R)),
            vm((1, R)),
            pltpu.SemaphoreType.DMA((NSEM,)),
            pltpu.SemaphoreType.DMA((NSEM,)),
            pltpu.SemaphoreType.DMA((6,)),
        ],
        compiler_params=pltpu.CompilerParams(
            collective_id=0, has_side_effects=True, vmem_limit_bytes=60 * 1024 * 1024
        ),
    )(flows, importer_factor, week_factor)
    return pl.pallas_call(
        hand_over,
        out_shape=shapes,
        in_specs=[pl.BlockSpec(memory_space=pl.ANY)] * 3,
        out_specs=[pl.BlockSpec(memory_space=pl.ANY)] * 3,
        scratch_shapes=[vm((ri, R)), vm((rj, R)), vm((1, R))] + [pltpu.SemaphoreType.DMA((PARTS + 2,))] * 2,
    )(*outs)


def solution(mesh):
    in_specs = (P("wk", "exp", "imp"), P("imp", None), P("wk", None))
    out_specs = (P("exp", None), P("imp", None), P("wk", None))
    fn = functools.partial(per_device, mesh.shape["exp"], mesh.shape["imp"] // 2, mesh.shape["wk"])
    return jax.shard_map(fn, mesh=mesh, in_specs=in_specs, out_specs=out_specs, check_vma=False)
```

```python
import functools

import jax
import jax.numpy as jnp
from jax import lax
from jax.experimental import pallas as pl
from jax.experimental.pallas import tpu as pltpu
from jax.sharding import PartitionSpec as P

ridge = 0.2
eps = 1e-06
hp = lax.Precision.HIGHEST
f32 = jnp.float32
bf16 = jnp.bfloat16
R = 256
H = 128
MESH = pl.DeviceIdType.MESH
STATS = 5
STEPS = 7


def dot(a, b, ca=1, cb=0):
    return lax.dot_general(a, b, (((ca,), (cb,)), ((), ())), precision=hp, preferred_element_type=f32)


def split(a):
    hi = a.astype(bf16)
    return hi, (a - hi.astype(f32)).astype(bf16)


def dot3(a, b):
    ah, al = a
    bh, bl = b
    d = functools.partial(jnp.dot, preferred_element_type=f32)
    return d(ah, bh) + (d(ah, bl) + d(al, bh))


def eye():
    return (lax.broadcasted_iota(jnp.int32, (R, R), 0) == lax.broadcasted_iota(jnp.int32, (R, R), 1)).astype(f32)


def nearly(h):
    one = eye()
    lam = ridge * jnp.sum(h * one) / R
    v = h + lam * one
    top = 1.0 + R / ridge
    alpha = 2.0 / (lam * (1.0 + top))
    delta = (top - 1.0) / (top + 1.0)
    e = one - alpha * v
    for step in range(STEPS):
        c = 2.0 / (2.0 - delta * delta)
        delta = delta * delta / (2.0 - delta * delta)
        se = split(e)
        x = (c * alpha) * (one + e) if step == 0 else c * (x + dot3(split(x), se))
        if step < STEPS - 1:
            e = c * dot3(se, se) + (1.0 - c) * one
    return v, x


def inverse(h):
    v, x = nearly(h)
    return x + dot3(split(x), split(eye() - dot(v, x)))


def solve(m, h):
    v, x = nearly(h)
    x = split(x)
    y = dot3(split(m), x)
    return y + dot3(split(m - dot(y, v)), x)


def triangle():
    r = lax.broadcasted_iota(jnp.int32, (H, H), 0)
    c = lax.broadcasted_iota(jnp.int32, (H, H), 1)
    return r, c


def pack(g):
    r, c = triangle()
    g11 = g[H:, H:]
    return jnp.where(r <= c, g[:H, :H], g11), g[:H, H:], jnp.sum(jnp.where(r == c, g11, 0.0), axis=0, keepdims=True)


def unpack(p0, p1, d):
    r, c = triangle()
    g00 = jnp.where(r <= c, p0, 0.0) + jnp.where(r < c, p0, 0.0).T
    low = jnp.where(r > c, p0, 0.0)
    g11 = low + low.T + jnp.where(r == c, d, 0.0)
    return jnp.concatenate(
        [jnp.concatenate([g00, p1], axis=1), jnp.concatenate([p1.T, g11], axis=1)], axis=0)


def kernel(ne, nz, nk, f_hbm, b_hbm, w_hbm, a_hbm, b_out_hbm, c_hbm,
           f_ref, b_ref, w_ref, fa, u, c_in, zb, vs, z_in, ma, cq, wx,
           pk, cs, ci, zi, xs, gi, gx, gag, mi, mo, mos, res, raw, a_out, b_out, c_out,
           ssem, rsem, lsem):
    e = lax.axis_index("exp")
    p = lax.axis_index("imp")
    k = lax.axis_index("wk")
    z = lax.div(p, 2)
    c = lax.rem(p, 2)
    o = 1 - c
    nq = ne * nk
    q = e * nk + k
    ri, rj = f_ref.shape
    yc = ri // nk
    zc = yc // nz
    jc = rj // nq
    gs = H // nq
    used = [0]
    pending = []

    loads = [pltpu.make_async_copy(f_hbm.at[0], f_ref, lsem.at[0]),
             pltpu.make_async_copy(b_hbm, b_ref, lsem.at[1]),
             pltpu.make_async_copy(w_hbm, w_ref, lsem.at[2])]
    for cp in loads:
        cp.start()
    stores = [pltpu.make_async_copy(src, dst, lsem.at[3 + i])
              for i, (src, dst) in enumerate([(a_out, a_hbm), (b_out, b_out_hbm), (c_out, c_hbm)])]

    def take():
        used[0] += 1
        return used[0] - 1

    def remote(src, dst, s, dev):
        return pltpu.make_async_remote_copy(
            src_ref=src, dst_ref=dst, send_sem=ssem.at[s], recv_sem=rsem.at[s],
            device_id=dev, device_id_type=MESH)

    core_dev = {"imp": z * 2 + o}

    def push_core(src, dst):
        cp = remote(src, dst, take(), core_dev)
        cp.start()
        pending.append(cp.wait_send)
        return cp.wait_recv

    def push_group(n, dev, src, dst, every, first=1):
        s = take()

        def go(i, carry):
            d = far(i, n)
            remote(src(d), dst, s, dev(d)).start()
            return carry

        lax.fori_loop(0, n - first, go, 0)
        cp = remote(every, every, s, dev(1))
        pending.append(cp.wait_send)
        return cp.wait_recv

    def push_both(n, dev, dev_o, src, src_o, dst, every, every_o):
        s, s_o = take(), take()

        def go(i, carry):
            d = far(i, n)
            remote(src(d), dst, s, dev(d)).start()
            remote(src_o(d), dst, s_o, dev_o(d)).start()
            return carry

        lax.fori_loop(0, n - 1, go, 0)
        remote(src_o(0), dst, s_o, dev_o(0)).start()
        cp = remote(every, every, s, dev(1))
        cp_o = remote(every_o, every_o, s_o, dev_o(0))
        pending.extend([cp.wait_send, cp_o.wait_send])

        def wait():
            cp.wait_recv()
            cp_o.wait_recv()

        return wait

    def far(i, n):
        h = lax.div(i + 1, 2)
        return lax.rem(n // 2 + jnp.where(lax.rem(i, 2) == 1, h, -h), n)

    def zto(d):
        return lax.rem(z + d, nz)

    def zdev(d):
        return {"imp": zto(d) * 2 + c}

    def zodev(d):
        return {"imp": zto(d) * 2 + o}

    def yto(d):
        return lax.rem(k + d, nk)

    def ydev(d):
        return {"wk": yto(d)}

    def qto(d):
        return lax.rem(q + d, nq)

    def qdev(d):
        return {"exp": lax.div(qto(d), nk), "wk": lax.rem(qto(d), nk)}

    def odev(d):
        return {"exp": lax.div(qto(d), nk), "wk": lax.rem(qto(d), nk), "imp": z * 2 + o}

    barrier = pltpu.get_barrier_semaphore()
    def greet(n, first, dev):
        def one_device(i, carry):
            pl.semaphore_signal(barrier, inc=1, device_id=dev(far(i, n)), device_id_type=MESH)
            return carry

        lax.fori_loop(0, n - first, one_device, 0)

    greet(nz, 1, zdev)
    greet(nz, 0, zodev)
    greet(nq, 1, qdev)
    greet(nq, 1, odev)

    def chain_fill(n, gram, stats):
        p0, p1, d = pack(gram)
        pk[0, :, :] = p0
        pk[1, :, :] = p1
        for h in range(2):
            cs[n, h, 0:gs, :] = pk[h, pl.ds(pl.multiple_of(q * gs, gs), gs), :]
            cs[n, h, gs:gs + 1, :] = d
            for s, row in enumerate(stats):
                cs[n, h, gs + 1 + s:gs + 2 + s, :] = row[:, h * H:(h + 1) * H]
            for s in range(len(stats), STATS - 1):
                cs[n, h, gs + 1 + s:gs + 2 + s, :] = jnp.zeros((1, H), f32)

    def chain_core(n):
        return push_core(cs.at[n, o], ci.at[n])

    def chain_z(n):
        zi[n, z, :, :] = cs[n, c] + ci[n]
        return push_group(nz, zdev, lambda d: zi.at[n, z], zi.at[n, z], zi.at[n, pl.ds(0, nz - 1)])

    def chain_q(n):
        xs[n, c, q, :, :] = jnp.sum(zi[n], axis=0)
        if n == 0:
            xs[n, c, q, gs + 1:gs + 2, :] = xs[n, c, q, gs + 1:gs + 2, :] + vs[c]
        mine = xs.at[n, c, q]
        return push_both(nq, qdev, odev, lambda d: mine, lambda d: mine, mine, xs.at[n, c, pl.ds(0, nq - 1)], xs.at[n, c])

    def chain_gram(n):
        return unpack(xs[n, 0, :, 0:gs, :].reshape(H, H), xs[n, 1, :, 0:gs, :].reshape(H, H), xs[n, 0, 0, gs:gs + 1, :])

    def chain_stat(n, qq, s):
        return jnp.concatenate([xs[n, h, qq, gs + 1 + s:gs + 2 + s, :] for h in range(2)], axis=1)

    def add(terms):
        tot = terms[0]
        for term in terms[1:]:
            tot = tot + term
        return tot

    for cp in loads:
        cp.wait()
    f = f_ref[...]
    b = b_ref[...]
    w = w_ref[...]
    own = jnp.sum(b, axis=0, keepdims=True) / rj
    shifted = b - own
    wx[k, :, :] = w
    rowp = dot(jnp.ones((8, rj), f32), f, 1, 1)
    colp = jnp.sum(f, axis=0, keepdims=True)
    cq[q, :, :] = colp
    zb[p, 0:1, :] = own
    zb[p, 1:2, :] = jnp.broadcast_to(jnp.sum(colp, axis=1, keepdims=True), (1, R))
    v = dot(jnp.broadcast_to(colp, (8, rj)), shifted)[0:1]
    chain_fill(0, dot(b, b, 0, 0), [v] + [rowp[0:1, i * R:(i + 1) * R] for i in range(ri // R)])
    fa[k, :, :] = f_ref[pl.ds(pl.multiple_of(k * yc, yc), yc), :]

    pl.semaphore_wait(barrier, (nz - 1) + nz + 2 * (nq - 1))

    w_zb = push_both(nz, zdev, zodev, lambda d: zb.at[p], lambda d: zb.at[p], zb.at[p],
                     zb.at[pl.ds(0, nz - 1)], zb.at[pl.ds(0, nz)])
    w_f = push_group(nk, ydev, lambda d: f_ref.at[pl.ds(pl.multiple_of(yto(d) * yc, yc), yc)], fa.at[k], fa.at[pl.ds(0, nk - 1)])
    w_cs = chain_core(0)
    w_w = push_group(nk, ydev, lambda d: wx.at[k], wx.at[k], wx.at[pl.ds(0, nk - 1)])
    w_cs()
    w_z = chain_z(0)
    w_c = push_group(nq, qdev, lambda d: cq.at[q], cq.at[q], cq.at[pl.ds(0, nq - 1)])

    w_w()
    ws = jnp.concatenate([wx[i] for i in range(nk)] + [jnp.zeros((8 - nk, R), f32)], axis=0)
    gram_c = dot(ws, ws, 0, 0)
    w_f()
    g = dot(fa[...].reshape(ri, rj), shifted)
    here = [jnp.sum(fa[i], axis=1, keepdims=True) for i in range(nk)]
    w_zb()
    means = zb[:, 0, :]
    mean = jnp.sum(means, axis=0, keepdims=True) / (2 * nz)
    off = own - mean
    moved = jnp.sum((means - mean) * zb[:, 1, :], axis=0, keepdims=True)
    vs[0, :, :] = moved[:, 0:H]
    vs[1, :, :] = moved[:, H:R]
    gw = add([(g[i * yc:(i + 1) * yc] + here[i] * off) * ws[i:i + 1] for i in range(nk)])
    u[0, :, :] = gw[:, 0:H]
    u[1, :, :] = gw[:, H:R]
    def cut(h, zz):
        return u.at[h, pl.ds(pl.multiple_of(zz * zc, zc), zc)]

    w_u = push_core(u.at[o], c_in)
    w_u()
    u[c, :, :] = u[c] + c_in[...]
    z_in[z, :, :] = cut(c, z)[...]
    w_z3 = push_group(nz, zdev, lambda d: cut(c, zto(d)), z_in.at[z], z_in.at[pl.ds(0, nz - 1)])
    w_z()
    w_q = chain_q(0)
    w_z3()
    tile = ma.at[c, pl.ds(pl.multiple_of(z * zc, zc), zc)]
    tile[...] = jnp.sum(z_in[...], axis=0)
    w_z4 = push_group(nz, zdev, lambda d: tile, tile, ma.at[c, pl.ds(0, yc - zc)])
    w_q()
    h1 = chain_gram(0) * gram_c
    one = eye()
    x1 = inverse(h1)

    w_c()
    zero = jnp.zeros((1, R), f32)
    pad = [jnp.zeros((1, H), f32)] * (8 - nk)
    seg, half = lax.div(k, 2), lax.rem(k, 2)
    coef, totals, cols = [], [], []
    for kk in range(nk):
        grand = add([jnp.sum(chain_stat(0, ee * nk + kk, 1 + i), axis=1, keepdims=True)
                     for ee in range(ne) for i in range(ri // R)])
        coef.append(add([chain_stat(0, ee * nk + kk, 0) for ee in range(ne)]) * ws[kk:kk + 1] / grand)
        totals.append(xs[0, half, e * nk + kk, pl.ds(gs + 2 + seg, 1), :])
        cols.append(add([cq[ee * nk + kk] for ee in range(ne)]) / grand)
    coef = jnp.concatenate(coef + [zero] * (8 - nk), axis=0)
    totals = jnp.concatenate(totals + pad, axis=0)
    week = lax.broadcasted_iota(jnp.int32, (8, 1), 0)
    fix = dot(totals, coef, 0, 0)

    w_z4()
    w_m = push_core(ma.at[c], ma.at[c])
    w_m()
    raw_a = dot(jnp.concatenate([ma[0], ma[1]], axis=1) - fix, x1)

    p0, p1, d = pack(dot(raw_a, raw_a, 0, 0))
    pk[0, :, :] = p0
    pk[1, :, :] = p1
    for i in range(nq):
        gx[i, 0:gs, :] = pk[c, i * gs:(i + 1) * gs, :]
        gx[i, gs:gs + 1, :] = d
    gi[q, :, :] = gx[q]
    w_gi = push_group(nq, qdev, lambda d: gx.at[qto(d)], gi.at[q], gi.at[pl.ds(0, nq - 1)])

    for kk in range(nk):
        only = (week == kk).astype(f32)
        res[:, kk * rj:(kk + 1) * rj] = fa[kk] - dot(totals * only, cols[kk] * only, 0, 0)
    t = dot(res[...], raw_a, 0, 0)
    tw = add([t[i * rj:(i + 1) * rj] * ws[i:i + 1] for i in range(nk)])
    for i in range(nq):
        mos[i, :, :] = tw[i * jc:(i + 1) * jc]
    mi[q, :, :] = mos[q]
    w_mi = push_group(nq, qdev, lambda d: mos.at[qto(d)], mi.at[q], mi.at[pl.ds(0, nq - 1)])
    raw[0, k, :, :] = raw_a[:, 0:H]
    raw[1, k, :, :] = raw_a[:, H:R]

    w_gi()
    gsum = jnp.sum(gi[...], axis=0)
    mine = gag.at[c, pl.ds(pl.multiple_of(q * gs, gs), gs)]
    mine[...] = gsum[0:gs]
    w_ga = push_both(nq, qdev, odev, lambda d: mine, lambda d: mine, mine, gag.at[c, pl.ds(0, H - gs)], gag.at[c])
    w_mi()
    mo[q, :, :] = jnp.sum(mi[...], axis=0)
    w_mo = push_group(nq, qdev, lambda d: mo.at[q], mo.at[q], mo.at[pl.ds(0, nq - 1)])
    w_ga()
    w_raw = push_group(nk, ydev, lambda d: raw.at[c, k], raw.at[c, k], raw.at[c, pl.ds(0, nk - 1)])
    gram_a = unpack(gag[0], gag[1], gsum[gs:gs + 1])

    def unscale(gram, count):
        d = gram * one
        inv_row = 1.0 / jnp.sqrt(jnp.sum(d, axis=0, keepdims=True) / count + eps)
        inv_col = 1.0 / jnp.sqrt(jnp.sum(d, axis=1, keepdims=True) / count + eps)
        return inv_row, gram * inv_row * inv_col

    sa, gram_a = unscale(gram_a, ri * ne)
    h2 = gram_a * gram_c
    w_mo()
    raw_b = solve(mo[...].reshape(rj, R) * sa, h2)

    chain_fill(1, dot(raw_b, raw_b, 0, 0),
               [jnp.sum(t[i * rj:(i + 1) * rj] * raw_b, axis=0, keepdims=True) for i in range(nk)])
    w_cs = chain_core(1)
    w_cs()
    w_z = chain_z(1)
    w_raw()
    w_rc = push_core(raw.at[c], raw.at[c])
    w_rc()
    a_out[:, 0:H] = raw[0].reshape(ri, H) * sa[:, 0:H]
    a_out[:, H:R] = raw[1].reshape(ri, H) * sa[:, H:R]
    stores[0].start()
    w_z()
    w_q = chain_q(1)
    w_q()
    sb, gram_b2 = unscale(chain_gram(1), rj * nz * 2)
    b_out[...] = raw_b * sb
    stores[1].start()
    h3 = gram_a * gram_b2
    scale = sa * sb
    m_c = jnp.concatenate([add([chain_stat(1, qq, kk) for qq in range(nq)]) * scale for kk in range(nk)] + [zero] * (8 - nk), axis=0)
    raw_c = solve(m_c, h3)
    sc = jnp.sqrt(jnp.sum(raw_c * raw_c, axis=0, keepdims=True) / nk + eps)
    c_out[...] = jnp.sum(raw_c * (week == k).astype(f32), axis=0, keepdims=True) / sc
    stores[2].start()

    for fin in pending:
        fin()
    for cp in stores:
        cp.wait()
    assert used[0] == NSEM


NSEM = 24
PARTS = 4


def hand_over(a_in, b_in, c_in, a_out, b_out, c_out, a, b, c, load, store):
    rows = a_in.shape[0] // PARTS
    steps = [(x_in.at[pl.ds(i * n, n)], x.at[pl.ds(i * n, n)], x_out.at[pl.ds(i * n, n)])
             for x_in, x, x_out, n, parts in ((a_in, a, a_out, rows, PARTS), (b_in, b, b_out, b_in.shape[0], 1))
             for i in range(parts)] + [(c_in, c, c_out)]
    loads = [pltpu.make_async_copy(src, mid, load.at[i]) for i, (src, mid, dst) in enumerate(steps)]
    stores = [pltpu.make_async_copy(mid, dst, store.at[i]) for i, (src, mid, dst) in enumerate(steps)]
    for cp in loads:
        cp.start()
    for first, then in zip(loads, stores):
        first.wait()
        then.start()
    for cp in stores:
        cp.wait()


def per_device(ne, nz, nk, flows, importer_factor, week_factor):
    ri, rj = flows.shape[1], flows.shape[2]
    nq = ne * nk
    gs = H // nq
    yc = ri // nk
    vm = functools.partial(pltpu.VMEM, dtype=f32)
    shapes = (
        jax.ShapeDtypeStruct((ri, R), f32),
        jax.ShapeDtypeStruct((rj, R), f32),
        jax.ShapeDtypeStruct((1, R), f32),
    )
    outs = pl.pallas_call(
        functools.partial(kernel, ne, nz, nk),
        out_shape=shapes,
        in_specs=[pl.BlockSpec(memory_space=pl.ANY)] * 3,
        out_specs=[pl.BlockSpec(memory_space=pl.ANY)] * 3,
        scratch_shapes=[
            vm((ri, rj)),
            vm((rj, R)),
            vm((1, R)),
            vm((nk, yc, rj)),
            vm((2, yc, H)),
            vm((yc, H)),
            vm((2 * nz, 2, R)),
            vm((2, 1, H)),
            vm((nz, yc // nz, H)),
            vm((2, yc, H)),
            vm((nq, 1, rj)),
            vm((nk, 1, R)),
            vm((2, H, H)),
            vm((2, 2, gs + STATS, H)),
            vm((2, gs + STATS, H)),
            vm((2, nz, gs + STATS, H)),
            vm((2, 2, nq, gs + STATS, H)),
            vm((nq, gs + 1, H)),
            vm((nq, gs + 1, H)),
            vm((2, H, H)),
            vm((nq, rj // nq, R)),
            vm((nq, rj // nq, R)),
            vm((nq, rj // nq, R)),
            vm((yc, nk * rj)),
            vm((2, nk, yc, H)),
            vm((ri, R)),
            vm((rj, R)),
            vm((1, R)),
            pltpu.SemaphoreType.DMA((NSEM,)),
            pltpu.SemaphoreType.DMA((NSEM,)),
            pltpu.SemaphoreType.DMA((6,)),
        ],
        compiler_params=pltpu.CompilerParams(
            collective_id=0, has_side_effects=True, vmem_limit_bytes=60 * 1024 * 1024
        ),
    )(flows, importer_factor, week_factor)
    return pl.pallas_call(
        hand_over,
        out_shape=shapes,
        in_specs=[pl.BlockSpec(memory_space=pl.ANY)] * 3,
        out_specs=[pl.BlockSpec(memory_space=pl.ANY)] * 3,
        scratch_shapes=[vm((ri, R)), vm((rj, R)), vm((1, R))] + [pltpu.SemaphoreType.DMA((PARTS + 2,))] * 2,
    )(*outs)


def solution(mesh):
    in_specs = (P("wk", "exp", "imp"), P("imp", None), P("wk", None))
    out_specs = (P("exp", None), P("imp", None), P("wk", None))
    fn = functools.partial(per_device, mesh.shape["exp"], mesh.shape["imp"] // 2, mesh.shape["wk"])
    return jax.shard_map(fn, mesh=mesh, in_specs=in_specs, out_specs=out_specs, check_vma=False)
```
